256 devices in a mesh: group: 8 (over x, core), region: 32 (over y, z).
Axes of the slice: x: 4, y: 4, z: 8, core: 2. Of those that a mesh axis runs over, the one named last changes fastest.
Arguments:
- positions: float32 [3, 4194304], P(None, ('group', 'region')), may hold values from -6 to 6
- velocities: float32 [3, 4194304], P(None, ('group', 'region')), may hold values from -6 to 6
- masses: float32 [4194304], P(('group', 'region')), may hold values from 0.0003 to 0.003
- smoothing: float32 [4194304], P(('group', 'region')), may hold values from 0.8 to 2.4
- energy: float32 [4194304], P(('group', 'region')), may hold values from 0.3 to 3
- density_old: float32 [4194304], P(('group', 'region')), may hold values from 0.3 to 3
- active_cells: int32 [256, 8], P(('group', 'region')), may hold values from 0 to 127, as said below
- active_count: int32 [256], P(('group', 'region')), may hold values from 1 to 8, as said below
- neighbours: int32 [256, 8, 26], P(('group', 'region')), may hold values from 0 to 207, as said below
- region_send: int32 [256, 32, 2], P(('group', 'region')), may hold values from 0 to 127
- group_send: int32 [256, 2, 8], P(('group', 'region')), may hold values from 0 to 127
Outputs:
- density_new: float32 [262144], P(('group', 'region'))
- acceleration: float32 [3, 262144], P(None, ('group', 'region'))
The draws below stay inside these ranges and needn't reach their ends.
Inputs may be any that keep to these rules, and one draw needn't show every extreme that they name: `active_cells`: on each device the slots name distinct cells. `active_count`: some device uses all 8 slots. `neighbours`: devices of the first group never name the positions of cells from the previous group, devices of the last group never those from the next group.
All inputs are finite; a program needn't handle non-finite values.
Results may differ from the reference program's by a relative error of at most 0.0003.
Values sent between devices are 32-bit elements; how exact they have to be, the bound alone decides.
A program may use at most 128 MiB of HBM per device.

```python
import math
import jax
import jax.numpy as jnp
from jax import lax

P_SIZE = 128
K = 26
S = 2
SG = 8
CD = 128
NA = 8
TB = 208
ROWS = 4194304
N_GROUP = 8
N_REGION = 32
DEVICES = 256


def draw_active_cells(key, part):
    key = jax.random.fold_in(key, 11)
    keys = jax.random.split(key, DEVICES)
    return jax.vmap(lambda one: jax.random.permutation(one, CD)[:NA])(keys).astype(jnp.int32)


def draw_active_count(key, part):
    key = jax.random.fold_in(key, 12)
    first, second = jax.random.split(key)
    counts = jax.random.randint(first, (DEVICES,), 1, NA + 1)
    busiest = jax.random.randint(second, (), 0, DEVICES)
    return jnp.where(jnp.arange(DEVICES) == busiest, NA, counts).astype(jnp.int32)


def draw_neighbours(key, part):
    key = jax.random.fold_in(key, 13)
    base = CD + N_REGION * S
    grp = jnp.arange(DEVICES) // N_REGION
    edge = ((grp == 0) | (grp == N_GROUP - 1))[:, None, None]
    raw = jax.random.randint(key, (DEVICES, NA, K), 0, TB)
    value = jnp.where(edge, raw % (TB - SG), raw)
    value = jnp.where((grp == 0)[:, None, None] & (value >= base), value + SG, value)
    return value.astype(jnp.int32)


def touch_ends(array, own_key, low, high):
    longest = array.shape.index(max(array.shape))
    spots = []
    for shift in (0, 1):
        where = [jax.random.randint(jax.random.fold_in(own_key, axis), (), 0, length) for axis, length in enumerate(array.shape)]
        where[longest] = (where[longest] + shift) % array.shape[longest]
        spots.append(tuple(where))
    return array.at[spots[0]].set(low).at[spots[1]].set(high)


def block_levels(rng, dims, pieces, least, top_value):
    gain = 1.0
    for axis_at, parts in pieces:
        heights = jax.random.uniform(jax.random.fold_in(jax.random.fold_in(rng, 6), axis_at), (parts,), jnp.float32, least / len(pieces), top_value / len(pieces))
        gain = gain * jnp.repeat(jnp.exp(heights), dims[axis_at] // parts).reshape((-1,) + (1,) * (len(dims) - 1 - axis_at))
    return gain


def scatter_about(rng, dims, scale, most, shards=(), kind=jnp.bfloat16):
    factor_of = block_levels(rng, dims, shards, -0.22, 0.18) if shards else 1.0
    array = jax.random.normal(rng, dims, jnp.float32) * scale * factor_of
    return jnp.minimum(jnp.maximum(array, -most), most).astype(kind)


def setup_inputs(seed: int = 0) -> dict:
    streams_of = jax.random.split(jax.random.key(seed), 12)
    positions = scatter_about(streams_of[0], (3, ROWS), 1.0, 6.0, ((1, 256),), jnp.float32)
    velocities = scatter_about(streams_of[1], (3, ROWS), 1.0, 6.0, ((1, 256),), jnp.float32)
    masses = jnp.clip(jnp.exp(math.log(0.003) - 2.3025851 * jax.random.uniform(streams_of[2], (ROWS,), jnp.float32) ** block_levels(streams_of[2], (ROWS,), ((0, 256),), -0.2, 0.2)), 0.0003, 0.003)
    smoothing = jnp.clip(jnp.exp(math.log(2.4) - 1.0986123 * jax.random.uniform(streams_of[3], (ROWS,), jnp.float32) ** block_levels(streams_of[3], (ROWS,), ((0, 256),), -0.2, 0.2)), 0.8, 2.4)
    energy = jnp.clip(jnp.exp(math.log(3.0) - 2.3025851 * jax.random.uniform(streams_of[4], (ROWS,), jnp.float32) ** block_levels(streams_of[4], (ROWS,), ((0, 256),), -0.2, 0.2)), 0.3, 3.0)
    density_old = jnp.clip(jnp.exp(math.log(3.0) - 2.3025851 * jax.random.uniform(streams_of[5], (ROWS,), jnp.float32) ** block_levels(streams_of[5], (ROWS,), ((0, 256),), -0.2, 0.2)), 0.3, 3.0)
    active_cells = draw_active_cells(jax.random.fold_in(streams_of[11], 71), 0)
    active_count = draw_active_count(jax.random.fold_in(streams_of[11], 71), 0)
    neighbours = draw_neighbours(jax.random.fold_in(streams_of[11], 71), 0)
    region_send = touch_ends(jax.random.randint(streams_of[9], (DEVICES, N_REGION, S), 0, CD), jax.random.fold_in(streams_of[9], 1), 0, CD - 1).astype(jnp.int32)
    group_send = touch_ends(jax.random.randint(streams_of[10], (DEVICES, 2, SG), 0, CD), jax.random.fold_in(streams_of[10], 1), 0, CD - 1).astype(jnp.int32)
    return dict(positions=positions, velocities=velocities, masses=masses, smoothing=smoothing, energy=energy, density_old=density_old, active_cells=active_cells, active_count=active_count, neighbours=neighbours, region_send=region_send, group_send=group_send)


step_time = 0.1
gas_factor = 2.0 / 3.0

def kernel_value(q, h):
    inner = jnp.where(q < 0.5, 1.0 - 6.0 * q * q + 6.0 * q * q * q, jnp.where(q < 1.0, 2.0 * (1.0 - q) ** 3, 0.0))
    return 8.0 / (math.pi * h ** 3) * inner

def kernel_slope(q, h):
    outer = -6.0 * (1.0 - q) ** 2 / jnp.maximum(q, 0.5)
    inner = jnp.where(q < 0.5, -12.0 + 18.0 * q, jnp.where(q < 1.0, outer, 0.0))
    return 8.0 / (math.pi * h ** 5) * inner

def geometry(table, cell, listed):
    index = jnp.concatenate([cell[None], listed]).astype(jnp.int32)
    other = jnp.take(table, index, axis=1)
    mine = other[:, 0]
    diff = mine[:3, None, :, None] - other[:3, :, None, :]
    dist = jnp.sqrt(lax.optimization_barrier(jnp.sum(diff * diff, axis=0)))
    width = mine[7][None, :, None]
    return (other, mine, diff, dist / width, width)

def density_one(table, cell, listed):
    other, mine, diff, q, width = geometry(table, cell, listed)
    return lax.optimization_barrier(jnp.sum(kernel_value(q, width) * other[6][:, None, :], axis=(0, 2)))

def force_one(table, cell, listed):
    other, mine, diff, q, width = geometry(table, cell, listed)
    coef = gas_factor * (mine[8] / mine[9])[None, :, None] + gas_factor * (other[8] / other[9])[:, None, :]
    scale = other[6][:, None, :] * coef * kernel_slope(q, width)
    return -lax.optimization_barrier(jnp.sum(scale[None] * diff, axis=(1, 3)))

def reference(positions, velocities, masses, smoothing, energy, density_old, active_cells, active_count, neighbours, region_send, group_send):
    drifted = positions + step_time * velocities
    fields = jnp.concatenate([drifted, velocities, masses[None], smoothing[None], energy[None], density_old[None]], 0)
    fields = fields.reshape(10, DEVICES, CD, P_SIZE)

    def table_for(dev, data):
        grp = dev // N_REGION
        pos = dev % N_REGION
        peers = grp * N_REGION + jnp.arange(N_REGION, dtype=jnp.int32)
        chosen = region_send[peers, pos]
        region_part = data[:, peers[:, None], chosen].reshape(data.shape[0], N_REGION * S, P_SIZE)
        prev_dev = jnp.maximum(dev - N_REGION, 0)
        next_dev = jnp.minimum(dev + N_REGION, DEVICES - 1)
        from_prev = jnp.where(grp > 0, data[:, prev_dev, group_send[prev_dev, 1]], 0.0)
        from_next = jnp.where(grp < N_GROUP - 1, data[:, next_dev, group_send[next_dev, 0]], 0.0)
        return jnp.concatenate([data[:, dev], region_part, from_prev, from_next], 1)
    slot_ids = jnp.arange(NA, dtype=jnp.int32)

    def density_device(dev):
        table = table_for(dev, fields)
        rho = lax.map(lambda pair: density_one(table, pair[0], pair[1]), (active_cells[dev], neighbours[dev]))
        return jnp.where((slot_ids < active_count[dev])[:, None], rho, 0.0)
    rho_all = lax.map(density_device, jnp.arange(DEVICES, dtype=jnp.int32))

    def update(dens, act, count, rho):
        cells = jnp.arange(CD, dtype=jnp.int32)
        for slot in range(NA):
            hit = (cells == act[slot]) & (slot < count)
            dens = jnp.where(hit[:, None], rho[slot][None, :], dens)
        return dens
    dens_all = jax.vmap(update)(fields[9], active_cells, active_count, rho_all)
    updated = fields.at[9].set(dens_all)

    def force_device(dev):
        table = table_for(dev, updated)
        acc = lax.map(lambda pair: force_one(table, pair[0], pair[1]), (active_cells[dev], neighbours[dev]))
        return jnp.where((slot_ids < active_count[dev])[:, None, None], acc, 0.0)
    acc_all = lax.map(force_device, jnp.arange(DEVICES, dtype=jnp.int32))
    density_new = rho_all.reshape(-1)
    acceleration = jnp.transpose(acc_all, (2, 0, 1, 3)).reshape(3, -1)
    return (density_new, acceleration)
```

```python
import functools
import math

import jax
import jax.numpy as jnp
from jax import lax
from jax.experimental import pallas as pl
from jax.experimental.pallas import tpu as pltpu
from jax.sharding import PartitionSpec as P

P_SIZE = 128
K = 26
S = 2
SG = 8
CD = 128
NA = 8
TB = 208
NL = K + 1
CH = 32
MESH = pl.DeviceIdType.MESH

step_time = 0.1
density_factor = 16.0 / math.pi
force_factor = 32.0 / math.pi
tiny = 1e-30


def lanes_to_rows(row):
    return jnp.transpose(jnp.broadcast_to(row, (P_SIZE, P_SIZE)))


def kernel(
    ng,
    nr,
    pos,
    vel,
    mass,
    smooth,
    energy,
    dens,
    act,
    cnt,
    nb,
    rsend,
    gsend,
    rho_out,
    acc_out,
    tbl,
    cells,
    send,
    ctbl,
    csend,
    cown,
    gbuf,
    own,
    part,
    rows,
    sems,
):
    g = lax.axis_index("group")
    r = lax.axis_index("region")
    up = lax.rem(g + 1, ng)
    down = lax.rem(g + ng - 1, ng)

    barrier = pltpu.get_barrier_semaphore()

    def greet(k, carry):
        pl.semaphore_signal(barrier, inc=1, device_id=(g, lax.rem(r + k, nr)), device_id_type=MESH)
        return carry

    lax.fori_loop(1, nr, greet, 0)
    pl.semaphore_signal(barrier, inc=1, device_id=(up, r), device_id_type=MESH)
    pl.semaphore_signal(barrier, inc=1, device_id=(down, r), device_id_type=MESH)

    def drifted(c):
        at = pl.ds(pl.multiple_of(c * P_SIZE, P_SIZE), P_SIZE)
        return pos[:, at] + step_time * vel[:, at]

    def gather(j, carry):
        for u in range(8):
            c = j * 8 + u
            cells[c, 0:3, :] = drifted(c)
            cells[c, 3:4, :] = mass[pl.ds(c, 1), :]
        return carry

    lax.fori_loop(0, CD // 8, gather, 0)

    def pack_region(j, carry):
        for s in range(S):
            send[j * S + s] = cells[rsend[0, j, s]]
        return carry

    def pack_group(j, carry):
        for side in range(2):
            send[nr * S + side * SG + j] = cells[gsend[0, side, j]]
        return carry

    lax.fori_loop(0, nr, pack_region, 0)
    lax.fori_loop(0, SG, pack_group, 0)

    pl.semaphore_wait(barrier, nr + 1)

    def region_copy(src, dst, sem, peer):
        return pltpu.make_async_remote_copy(
            src_ref=src.at[pl.ds(peer * S, S)],
            dst_ref=dst.at[pl.ds(CD + r * S, S)],
            send_sem=sems.at[sem],
            recv_sem=sems.at[sem + 1],
            device_id=(g, peer),
            device_id_type=MESH,
        )

    def group_copy(src, dst, sem, side):
        return pltpu.make_async_remote_copy(
            src_ref=src.at[pl.ds(nr * S + side * SG, SG)],
            dst_ref=dst.at[pl.ds(CD + nr * S + (1 - side) * SG, SG)],
            send_sem=sems.at[sem + 2 + 2 * side],
            recv_sem=sems.at[sem + 3 + 2 * side],
            device_id=(up if side else down, r),
            device_id_type=MESH,
        )

    def start_all(src, dst, sem):
        def go(k, carry):
            region_copy(src, dst, sem, lax.rem(r + k, nr)).start()
            return carry

        lax.fori_loop(1, nr, go, 0)
        group_copy(src, dst, sem, 0).start()
        group_copy(src, dst, sem, 1).start()

    def wait_all(src, dst, sem):
        whole = pltpu.make_async_remote_copy(
            src_ref=src.at[pl.ds(0, (nr - 1) * S)],
            dst_ref=dst.at[pl.ds(CD, (nr - 1) * S)],
            send_sem=sems.at[sem],
            recv_sem=sems.at[sem + 1],
            device_id=(g, lax.rem(r + 1, nr)),
            device_id_type=MESH,
        )
        whole.wait_send()
        whole.wait_recv()
        for side in range(2):
            one = group_copy(src, dst, sem, side)
            one.wait_send()
            one.wait_recv()

    start_all(send, tbl, 0)

    tbl[pl.ds(CD + r * S, S)] = send[pl.ds(r * S, S)]

    def fill(j, carry):
        at = pl.ds(j * 8, 8)
        tbl[at] = cells[at]
        return carry

    lax.fori_loop(0, CD // 8, fill, 0)

    def own_rows(i, carry):
        a = act[0, i]
        d = cells[a]
        h = smooth[pl.ds(a, 1), :]
        for f in range(3):
            own[i, f] = lanes_to_rows(d[f : f + 1])
        own[i, 3] = lanes_to_rows(h)
        return carry

    lax.fori_loop(0, NA, own_rows, 0)
    wait_all(send, tbl, 0)

    def index_of(i, k):
        return act[0, i] if k == 0 else nb[0, i, k - 1]

    def density(step, carry):
        i = step // (P_SIZE // CH)
        at = pl.ds(pl.multiple_of(lax.rem(step, P_SIZE // CH) * CH, CH), CH)
        x, y, z, h = (own[i, f, at, :] for f in range(4))
        hh = 0.5 * h
        total = jnp.zeros((CH, P_SIZE), jnp.float32)
        for k in range(NL):
            other = tbl[index_of(i, k)]
            dx = x - other[0:1]
            dy = y - other[1:2]
            dz = z - other[2:3]
            m = other[3:4]
            d2 = jnp.maximum(dx * dx + dy * dy + dz * dz, tiny)
            inv = lax.rsqrt(d2)
            d = d2 * inv
            t = jnp.maximum(h - d, 0.0)
            v = jnp.maximum(hh - d, 0.0)
            t2 = t * t
            v4 = 4.0 * (v * v)
            total += m * (t2 * t - v4 * v)
            gbuf[i * NL + k, at, :] = m * ((t2 - v4) * inv)
        part[0, i, at, :] = total
        return carry

    lax.fori_loop(0, NA * (P_SIZE // CH), density, 0)

    def column_sums(block):
        return jnp.sum(jnp.transpose(block), axis=0, keepdims=True)

    count = jnp.full((1, P_SIZE), cnt[0], jnp.int32)
    fresh = dens[...]
    ids = lax.broadcasted_iota(jnp.int32, (CD, P_SIZE), 0)
    for i in range(NA):
        used = count > i
        h = smooth[pl.ds(act[0, i], 1), :]
        h3 = h * h * h
        rho = density_factor / (h3 * h3) * column_sums(part[0, i])
        rho_out[i : i + 1, :] = jnp.where(used, rho, 0.0)
        fresh = jnp.where((ids == act[0, i]) & used, rho, fresh)
        rows[i : i + 1, :] = rho
    cown[...] = energy[...] / fresh

    def pack2(j, carry):
        for s in range(S):
            csend[j * S + s] = cown[pl.ds(rsend[0, j, s], 1), :]
        return carry

    def pack2_group(j, carry):
        for side in range(2):
            csend[nr * S + side * SG + j] = cown[pl.ds(gsend[0, side, j], 1), :]
        return carry

    lax.fori_loop(0, nr, pack2, 0)
    lax.fori_loop(0, SG, pack2_group, 0)
    start_all(csend, ctbl, 6)

    ctbl[pl.ds(CD + r * S, S)] = csend[pl.ds(r * S, S)]

    def fill2(j, carry):
        for u in range(8):
            ctbl[j * 8 + u] = cown[pl.ds(j * 8 + u, 1), :]
        return carry

    lax.fori_loop(0, CD // 8, fill2, 0)

    def own_ratio(i, carry):
        u = energy[pl.ds(act[0, i], 1), :]
        own[i, 3] = lanes_to_rows(u / rows[pl.ds(i, 1), :])
        return carry

    lax.fori_loop(0, NA, own_ratio, 0)
    wait_all(csend, ctbl, 6)

    def force(step, carry):
        i = step // (P_SIZE // CH)
        at = pl.ds(pl.multiple_of(lax.rem(step, P_SIZE // CH) * CH, CH), CH)
        x, y, z, c = (own[i, f, at, :] for f in range(4))
        ax = ay = az = jnp.zeros((CH, P_SIZE), jnp.float32)
        for k in range(NL):
            index = index_of(i, k)
            other = tbl[index]
            w = gbuf[i * NL + k, at, :] * (c + ctbl[index])
            ax += w * (x - other[0:1])
            ay += w * (y - other[1:2])
            az += w * (z - other[2:3])
        part[0, i, at, :] = ax
        part[1, i, at, :] = ay
        part[2, i, at, :] = az
        return carry

    lax.fori_loop(0, NA * (P_SIZE // CH), force, 0)

    for i in range(NA):
        used = count > i
        h = smooth[pl.ds(act[0, i], 1), :]
        h3 = h * h * h
        scale = force_factor / (h3 * h3)
        for f in range(3):
            acc_out[f : f + 1, i * P_SIZE : (i + 1) * P_SIZE] = jnp.where(
                used, scale * column_sums(part[f, i]), 0.0
            )


def body(pos, vel, mass, smooth, energy, dens, act, cnt, nb, rsend, gsend):
    ng, nr = lax.axis_size("group"), lax.axis_size("region")
    square = lambda v: v.reshape(CD, P_SIZE)
    vmem = pl.BlockSpec(memory_space=pltpu.VMEM)
    smem = pl.BlockSpec(memory_space=pltpu.SMEM)
    f32 = jnp.float32
    rho, acc = pl.pallas_call(
        functools.partial(kernel, ng, nr),
        out_shape=(
            jax.ShapeDtypeStruct((NA, P_SIZE), f32),
            jax.ShapeDtypeStruct((3, NA * P_SIZE), f32),
        ),
        in_specs=[vmem] * 6 + [smem] * 5,
        out_specs=(vmem, vmem),
        scratch_shapes=[
            pltpu.VMEM((TB, 4, P_SIZE), f32),
            pltpu.VMEM((CD, 4, P_SIZE), f32),
            pltpu.VMEM((nr * S + 2 * SG, 4, P_SIZE), f32),
            pltpu.VMEM((TB, 1, P_SIZE), f32),
            pltpu.VMEM((nr * S + 2 * SG, 1, P_SIZE), f32),
            pltpu.VMEM((CD, P_SIZE), f32),
            pltpu.VMEM((NA * NL, P_SIZE, P_SIZE), f32),
            pltpu.VMEM((NA, 4, P_SIZE, P_SIZE), f32),
            pltpu.VMEM((3, NA, P_SIZE, P_SIZE), f32),
            pltpu.VMEM((NA, P_SIZE), f32),
            pltpu.SemaphoreType.DMA((12,)),
        ],
        compiler_params=pltpu.CompilerParams(
            collective_id=0, has_side_effects=True, vmem_limit_bytes=48 * 1024 * 1024
        ),
    )(pos, vel, square(mass), square(smooth), square(energy), square(dens), act, cnt, nb, rsend, gsend)
    return rho.reshape(-1), acc


def solution(mesh):
    both = ("group", "region")
    placed = (
        P(None, both),
        P(None, both),
        P(both),
        P(both),
        P(both),
        P(both),
        P(both, None),
        P(both),
        P(both, None, None),
        P(both, None, None),
        P(both, None, None),
    )
    return jax.shard_map(
        body,
        mesh=mesh,
        in_specs=placed,
        out_specs=(P(both), P(None, both)),
        check_vma=False,
    )
```

```python
import functools
import math

import jax
import jax.numpy as jnp
from jax import lax
from jax.experimental import pallas as pl
from jax.experimental.pallas import tpu as pltpu
from jax.sharding import PartitionSpec as P

P_SIZE = 128
K = 26
S = 2
SG = 8
CD = 128
NA = 8
TB = 208
NL = K + 1
MESH = pl.DeviceIdType.MESH

step_time = 0.1
density_factor = 16.0 / math.pi
force_factor = 32.0 / math.pi
tiny = 1e-30


def lanes_to_rows(row):
    return jnp.transpose(jnp.broadcast_to(row, (P_SIZE, P_SIZE)))


def three_parts(value):
    first = value.astype(jnp.bfloat16).astype(jnp.float32)
    rest = value - first
    second = rest.astype(jnp.bfloat16).astype(jnp.float32)
    return first, second, rest - second


def square_length(cell):
    sq = cell * cell
    return sq[0:1] + sq[1:2] + sq[2:3]


def kernel(
    ng,
    nr,
    pos_in,
    vel_in,
    mass_in,
    smooth_in,
    energy_in,
    dens_in,
    act_in,
    cnt_in,
    nb_in,
    rsend_in,
    gsend_in,
    rho_out,
    acc_out,
    pos,
    vel,
    mass,
    smooth,
    energy,
    dens,
    act,
    cnt,
    nb,
    rsend,
    gsend,
    tbl,
    cells,
    send,
    ctbl,
    csend,
    cown,
    rhs,
    lhs,
    weights,
    hbuf,
    part,
    rows,
    dbuf,
    ibuf,
    gbuf,
    in_sems,
    sems,
):
    g = lax.axis_index("group")
    r = lax.axis_index("region")
    up = lax.rem(g + 1, ng)
    down = lax.rem(g + ng - 1, ng)
    ny, nz = nr // 8, 8

    loads = [
        pltpu.make_async_copy(src, dst, in_sems.at[n])
        for n, (src, dst) in enumerate(
            (
                (pos_in, pos),
                (vel_in, vel),
                (mass_in, mass),
                (rsend_in, rsend),
                (gsend_in, gsend),
                (smooth_in, smooth),
                (act_in, act),
                (nb_in, nb),
                (energy_in, energy),
                (dens_in, dens),
                (cnt_in, cnt),
            )
        )
    ]
    for load in loads:
        load.start()

    def far_to_near(k):
        a, b = lax.div(k, ny), lax.rem(k, ny)
        dz = nz // 2 + lax.div(a + 1, 2) * (1 - 2 * lax.rem(a, 2))
        dy = ny // 2 + lax.div(b + 1, 2) * (1 - 2 * lax.rem(b, 2))
        y, z = lax.div(r, nz), lax.rem(r, nz)
        return lax.rem(y + dy, ny) * nz + lax.rem(z + dz, nz)

    barrier = pltpu.get_barrier_semaphore()

    def greet(k, carry):
        pl.semaphore_signal(barrier, inc=1, device_id=(g, far_to_near(k)), device_id_type=MESH)
        return carry

    lax.fori_loop(0, nr - 1, greet, 0)
    pl.semaphore_signal(barrier, inc=1, device_id=(up, r), device_id_type=MESH)
    pl.semaphore_signal(barrier, inc=1, device_id=(down, r), device_id_type=MESH)

    def drifted(c):
        at = pl.ds(pl.multiple_of(c * P_SIZE, P_SIZE), P_SIZE)
        return pos[:, at] + step_time * vel[:, at]

    def gather(j, carry):
        for u in range(8):
            c = j * 8 + u
            cells[c, 0:3, :] = drifted(c)
            cells[c, 3:4, :] = mass[pl.ds(c, 1), :]
        return carry

    for load in loads[:5]:
        load.wait()
    lax.fori_loop(0, CD // 8, gather, 0)

    def pack_region(j, carry):
        for s in range(S):
            send[j * S + s] = cells[rsend[0, j, s]]
        return carry

    def pack_group(j, carry):
        for side in range(2):
            send[nr * S + side * SG + j] = cells[gsend[0, side, j]]
        return carry

    lax.fori_loop(0, nr, pack_region, 0)
    lax.fori_loop(0, SG, pack_group, 0)

    pl.semaphore_wait(barrier, nr + 1)

    def region_copy(src, dst, sem, peer):
        return pltpu.make_async_remote_copy(
            src_ref=src.at[pl.ds(peer * S, S)],
            dst_ref=dst.at[pl.ds(CD + r * S, S)],
            send_sem=sems.at[sem],
            recv_sem=sems.at[sem + 1],
            device_id=(g, peer),
            device_id_type=MESH,
        )

    def group_copy(src, dst, sem, side):
        return pltpu.make_async_remote_copy(
            src_ref=src.at[pl.ds(nr * S + side * SG, SG)],
            dst_ref=dst.at[pl.ds(CD + nr * S + (1 - side) * SG, SG)],
            send_sem=sems.at[sem + 2 + 2 * side],
            recv_sem=sems.at[sem + 3 + 2 * side],
            device_id=(up if side else down, r),
            device_id_type=MESH,
        )

    def start_all(src, dst, sem):
        def go(k, carry):
            region_copy(src, dst, sem, far_to_near(k)).start()
            return carry

        lax.fori_loop(0, nr - 1, go, 0)
        group_copy(src, dst, sem, 0).start()
        group_copy(src, dst, sem, 1).start()

    def wait_all(src, dst, sem):
        whole = pltpu.make_async_remote_copy(
            src_ref=src.at[pl.ds(0, (nr - 1) * S)],
            dst_ref=dst.at[pl.ds(CD, (nr - 1) * S)],
            send_sem=sems.at[sem],
            recv_sem=sems.at[sem + 1],
            device_id=(g, lax.rem(r + 1, nr)),
            device_id_type=MESH,
        )
        whole.wait_send()
        whole.wait_recv()
        for side in range(2):
            one = group_copy(src, dst, sem, side)
            one.wait_send()
            one.wait_recv()

    start_all(send, tbl, 0)

    tbl[pl.ds(CD + r * S, S)] = send[pl.ds(r * S, S)]

    def fill(j, carry):
        at = pl.ds(j * 8, 8)
        tbl[at] = cells[at]
        return carry

    lax.fori_loop(0, CD // 8, fill, 0)
    for load in loads[5:]:
        load.wait()

    one_row = jnp.ones((1, P_SIZE), jnp.float32)
    zero_rows = jnp.zeros((3, P_SIZE), jnp.float32)

    def partner_factors(cell):
        a, b, c = three_parts(
            jnp.concatenate([cell[0:3], square_length(cell), one_row, zero_rows], axis=0)
        )
        return jnp.concatenate([a, b, c, a, b, a], axis=0).astype(jnp.bfloat16)

    def own_factors(j, carry):
        for u in range(4):
            rhs[j * 4 + u] = partner_factors(cells[j * 4 + u])
        return carry

    lax.fori_loop(0, CD // 4, own_factors, 0)

    def own_rows(i, carry):
        at = act[0, i]
        cell = cells[at]
        a, b, c = three_parts(
            jnp.concatenate([-2.0 * cell[0:3], one_row, square_length(cell), zero_rows], axis=0)
        )
        wide = jnp.concatenate(
            [a, a, a, b, b, c, jnp.zeros((P_SIZE - 48, P_SIZE), jnp.float32)], axis=0
        )
        lhs[i] = jnp.transpose(wide)[:, 0:48].astype(jnp.bfloat16)
        h = lanes_to_rows(smooth[pl.ds(at, 1), :])
        hbuf[0, i] = h
        hbuf[1, i] = 0.5 * (h * h * h)
        return carry

    lax.fori_loop(0, NA, own_rows, 0)

    def density_of(i, k, square, m):
        h = hbuf[0, i]
        square = jnp.maximum(square, tiny)
        inv = lax.rsqrt(square)
        d = square * inv
        t = jnp.maximum(h - d, 0.0)
        dbuf[i * NL + k] = d
        ibuf[i * NL + k] = inv
        return m * jnp.minimum(t * t * t, hbuf[1, i] - 3.0 * (square * t))

    def density_self(i, carry):
        at = act[0, i]
        square = jnp.dot(lhs[i], rhs[at], preferred_element_type=jnp.float32)
        part[i] = density_of(i, 0, square, cells[at][3:4])
        return carry

    lax.fori_loop(0, NA, density_self, 0)
    wait_all(send, tbl, 0)

    def other_factors(j, carry):
        for u in range(4):
            c = CD + j * 4 + u
            rhs[c] = partner_factors(tbl[c])
        return carry

    lax.fori_loop(0, (TB - CD) // 4, other_factors, 0)

    def density(i, carry):
        total = part[i]
        for k in range(1, NL, 2):
            first, second = nb[0, i, k - 1], nb[0, i, k]
            square = jnp.dot(
                lhs[i],
                jnp.concatenate([rhs[first], rhs[second]], axis=1),
                preferred_element_type=jnp.float32,
            )
            total += density_of(i, k, square[:, :P_SIZE], tbl[first][3:4])
            total += density_of(i, k + 1, square[:, P_SIZE:], tbl[second][3:4])
        part[i] = total
        return carry

    lax.fori_loop(0, NA, density, 0)

    count = jnp.full((1, P_SIZE), cnt[0], jnp.int32)
    fresh = dens[...]
    ids = lax.broadcasted_iota(jnp.int32, (CD, P_SIZE), 0)
    for i in range(NA):
        used = count > i
        h = smooth[pl.ds(act[0, i], 1), :]
        h3 = h * h * h
        rho = density_factor / (h3 * h3) * jnp.sum(jnp.transpose(part[i]), axis=0, keepdims=True)
        rho_out[i : i + 1, :] = jnp.where(used, rho, 0.0)
        fresh = jnp.where((ids == act[0, i]) & used, rho, fresh)
        rows[i : i + 1, :] = rho
    cown[...] = energy[...] / fresh

    def pack2(j, carry):
        for s in range(S):
            csend[j * S + s] = cown[pl.ds(rsend[0, j, s], 1), :]
        return carry

    def pack2_group(j, carry):
        for side in range(2):
            csend[nr * S + side * SG + j] = cown[pl.ds(gsend[0, side, j], 1), :]
        return carry

    lax.fori_loop(0, nr, pack2, 0)
    lax.fori_loop(0, SG, pack2_group, 0)
    start_all(csend, ctbl, 6)

    ctbl[pl.ds(CD + r * S, S)] = csend[pl.ds(r * S, S)]

    def partner_weights(cell, ratio):
        base = cell[3:4] * jnp.concatenate([one_row, cell[0:3]], axis=0)
        a, b, c = three_parts(jnp.concatenate([base, base * ratio], axis=0))
        return jnp.concatenate([a, b, c, jnp.zeros_like(a)], axis=0).astype(jnp.bfloat16)

    def own_weights(j, carry):
        for u in range(4):
            c = j * 4 + u
            weights[c] = partner_weights(cells[c], cown[pl.ds(c, 1), :])
        return carry

    lax.fori_loop(0, CD // 4, own_weights, 0)

    def slope(step, carry):
        i = lax.div(step, NL)
        d = dbuf[step]
        t = jnp.maximum(hbuf[0, i] - d, 0.0)
        value = jnp.where(t > d, t + t - d, t * t * ibuf[step])
        a = value.astype(jnp.bfloat16)
        rest = value - a.astype(jnp.float32)
        b = rest.astype(jnp.bfloat16)
        gbuf[0, step] = a
        gbuf[1, step] = b
        gbuf[2, step] = (rest - b.astype(jnp.float32)).astype(jnp.bfloat16)
        return carry

    lax.fori_loop(0, NA * NL, slope, 0)
    wait_all(csend, ctbl, 6)

    def other_weights(j, carry):
        for u in range(4):
            c = CD + j * 4 + u
            weights[c] = partner_weights(tbl[c], ctbl[c])
        return carry

    lax.fori_loop(0, (TB - CD) // 4, other_weights, 0)

    def force(i, carry):
        total = jnp.zeros((P_SIZE, 32), jnp.float32)
        for k in range(NL):
            w = weights[act[0, i] if k == 0 else nb[0, i, k - 1]]
            for n in range(3):
                total += lax.dot_general(
                    gbuf[n, i * NL + k],
                    w,
                    (((1,), (1,)), ((), ())),
                    preferred_element_type=jnp.float32,
                )
        part[i, :, 0:32] = total
        return carry

    lax.fori_loop(0, NA, force, 0)

    for i in range(NA):
        used = count > i
        at = act[0, i]
        cell = cells[at]
        h = smooth[pl.ds(at, 1), :]
        h3 = h * h * h
        scale = force_factor / (h3 * h3)
        ratio = energy[pl.ds(at, 1), :] / rows[i : i + 1, :]
        sums = jnp.transpose(part[i])
        sums = sums[0:8] + sums[8:16] + sums[16:24]
        for f in range(3):
            x = cell[f : f + 1]
            mine = x * sums[0:1] - sums[f + 1 : f + 2]
            theirs = x * sums[4:5] - sums[f + 5 : f + 6]
            acc_out[f : f + 1, i * P_SIZE : (i + 1) * P_SIZE] = jnp.where(
                used, scale * (ratio * mine + theirs), 0.0
            )


def body(pos, vel, mass, smooth, energy, dens, act, cnt, nb, rsend, gsend):
    ng, nr = lax.axis_size("group"), lax.axis_size("region")
    square = lambda v: v.reshape(CD, P_SIZE)
    hbm = pl.BlockSpec(memory_space=pltpu.HBM)
    vmem = pl.BlockSpec(memory_space=pltpu.VMEM)
    f32, b16 = jnp.float32, jnp.bfloat16
    args = (pos, vel, square(mass), square(smooth), square(energy), square(dens), act, cnt, nb, rsend, gsend)
    held = [pltpu.VMEM(v.shape, f32) for v in args[:6]] + [pltpu.SMEM(v.shape, jnp.int32) for v in args[6:]]
    sent = nr * S + 2 * SG
    rho, acc = pl.pallas_call(
        functools.partial(kernel, ng, nr),
        out_shape=(
            jax.ShapeDtypeStruct((NA, P_SIZE), f32),
            jax.ShapeDtypeStruct((3, NA * P_SIZE), f32),
        ),
        in_specs=[hbm] * len(args),
        out_specs=(vmem, vmem),
        scratch_shapes=held
        + [
            pltpu.VMEM((TB, 4, P_SIZE), f32),
            pltpu.VMEM((CD, 4, P_SIZE), f32),
            pltpu.VMEM((sent, 4, P_SIZE), f32),
            pltpu.VMEM((TB, 1, P_SIZE), f32),
            pltpu.VMEM((sent, 1, P_SIZE), f32),
            pltpu.VMEM((CD, P_SIZE), f32),
            pltpu.VMEM((TB, 48, P_SIZE), b16),
            pltpu.VMEM((NA, P_SIZE, 48), b16),
            pltpu.VMEM((TB, 32, P_SIZE), b16),
            pltpu.VMEM((2, NA, P_SIZE, P_SIZE), f32),
            pltpu.VMEM((NA, P_SIZE, P_SIZE), f32),
            pltpu.VMEM((NA, P_SIZE), f32),
            pltpu.VMEM((NA * NL, P_SIZE, P_SIZE), f32),
            pltpu.VMEM((NA * NL, P_SIZE, P_SIZE), f32),
            pltpu.VMEM((3, NA * NL, P_SIZE, P_SIZE), b16),
            pltpu.SemaphoreType.DMA((len(args),)),
            pltpu.SemaphoreType.DMA((12,)),
        ],
        compiler_params=pltpu.CompilerParams(
            collective_id=0, has_side_effects=True, vmem_limit_bytes=62 * 1024 * 1024
        ),
    )(*args)
    return rho.reshape(-1), acc


def solution(mesh):
    both = ("group", "region")
    placed = (
        P(None, both),
        P(None, both),
        P(both),
        P(both),
        P(both),
        P(both),
        P(both, None),
        P(both),
        P(both, None, None),
        P(both, None, None),
        P(both, None, None),
    )
    return jax.shard_map(
        body,
        mesh=mesh,
        in_specs=placed,
        out_specs=(P(both), P(None, both)),
        check_vma=False,
    )
```

```python
import functools
import math

import jax
import jax.numpy as jnp
from jax import lax
from jax.experimental import pallas as pl
from jax.experimental.pallas import tpu as pltpu
from jax.sharding import PartitionSpec as P

P_SIZE = 128
K = 26
S = 2
SG = 8
CD = 128
NA = 8
TB = 208
NL = K + 1
MESH = pl.DeviceIdType.MESH

step_time = 0.1
density_factor = 16.0 / math.pi
force_factor = 32.0 / math.pi
tiny = 1e-30


def lanes_to_rows(row):
    return jnp.transpose(jnp.broadcast_to(row, (P_SIZE, P_SIZE)))


def three_parts(value):
    first = value.astype(jnp.bfloat16).astype(jnp.float32)
    rest = value - first
    second = rest.astype(jnp.bfloat16).astype(jnp.float32)
    return first, second, rest - second


def square_length(cell):
    sq = cell * cell
    return sq[0:1] + sq[1:2] + sq[2:3]


def kernel(
    ng,
    nr,
    pos_in,
    vel_in,
    mass_in,
    smooth_in,
    energy_in,
    dens_in,
    act_in,
    cnt_in,
    nb_in,
    rsend_in,
    gsend_in,
    rho_out,
    acc_out,
    tbl,
    ctbl,
    flags,
    mine,
    nb_out,
    pos,
    vel,
    mass,
    smooth,
    energy,
    dens,
    act,
    cnt,
    nb,
    rsend,
    gsend,
    listed,
    cells,
    send,
    ctbl0,
    csend0,
    csend,
    cown,
    rhs,
    lhs,
    weights,
    hbuf,
    part,
    rows,
    dbuf,
    ibuf,
    in_sems,
    sems,
):
    g = lax.axis_index("group")
    r = lax.axis_index("region")
    up = lax.rem(g + 1, ng)
    down = lax.rem(g + ng - 1, ng)
    ny, nz = nr // 8, 8

    loads = [
        pltpu.make_async_copy(src, dst, in_sems.at[n])
        for n, (src, dst) in enumerate(
            (
                (pos_in, pos),
                (vel_in, vel),
                (mass_in, mass),
                (rsend_in, rsend),
                (gsend_in, gsend),
                (energy_in, energy),
                (dens_in, dens),
                (act_in, act),
                (cnt_in, cnt),
                (smooth_in, smooth),
                (nb_in, nb),
                (nb_in, nb_out),
            )
        )
    ]
    for load in loads:
        load.start()

    def far_to_near(k):
        a, b = lax.div(k, ny), lax.rem(k, ny)
        dz = nz // 2 + lax.div(a + 1, 2) * (1 - 2 * lax.rem(a, 2))
        dy = ny // 2 + lax.div(b + 1, 2) * (1 - 2 * lax.rem(b, 2))
        y, z = lax.div(r, nz), lax.rem(r, nz)
        return lax.rem(y + dy, ny) * nz + lax.rem(z + dz, nz)

    barrier = pltpu.get_barrier_semaphore()

    def greet(k, carry):
        pl.semaphore_signal(barrier, inc=1, device_id=(g, far_to_near(k)), device_id_type=MESH)
        return carry

    lax.fori_loop(0, nr - 1, greet, 0)
    pl.semaphore_signal(barrier, inc=1, device_id=(up, r), device_id_type=MESH)
    pl.semaphore_signal(barrier, inc=1, device_id=(down, r), device_id_type=MESH)

    def drifted(c):
        at = pl.ds(pl.multiple_of(c * P_SIZE, P_SIZE), P_SIZE)
        return pos[:, at] + step_time * vel[:, at]

    def gather(j, carry):
        for u in range(8):
            c = j * 8 + u
            cells[c, 0:3, :] = drifted(c)
            cells[c, 3:4, :] = mass[pl.ds(c, 1), :]
        return carry

    for load in loads[:5]:
        load.wait()
    lax.fori_loop(0, CD // 8, gather, 0)

    def pack_region(j, carry):
        for s in range(S):
            send[j * S + s] = cells[rsend[0, s, j]]
        return carry

    def pack_group(j, carry):
        for side in range(2):
            send[nr * S + side * SG + j] = cells[gsend[0, side, j]]
        return carry

    lax.fori_loop(0, nr, pack_region, 0)
    lax.fori_loop(0, SG, pack_group, 0)

    pl.semaphore_wait(barrier, nr + 1)

    def base(table):
        return table.shape[0] - nr * S - 2 * SG

    def region_copy(src, dst, sem, peer):
        return pltpu.make_async_remote_copy(
            src_ref=src.at[pl.ds(peer * S, S)],
            dst_ref=dst.at[pl.ds(base(dst) + r * S, S)],
            send_sem=sems.at[sem],
            recv_sem=sems.at[sem + 1],
            device_id=(g, peer),
            device_id_type=MESH,
        )

    def group_copy(src, dst, sem, side):
        return pltpu.make_async_remote_copy(
            src_ref=src.at[pl.ds(nr * S + side * SG, SG)],
            dst_ref=dst.at[pl.ds(base(dst) + nr * S + (1 - side) * SG, SG)],
            send_sem=sems.at[sem + 2 + 2 * side],
            recv_sem=sems.at[sem + 3 + 2 * side],
            device_id=(up if side else down, r),
            device_id_type=MESH,
        )

    def start_all(src, dst, sem):
        def go(k, carry):
            region_copy(src, dst, sem, far_to_near(k)).start()
            return carry

        lax.fori_loop(0, nr - 1, go, 0)
        group_copy(src, dst, sem, 0).start()
        group_copy(src, dst, sem, 1).start()

    def wait_all(src, dst, sem):
        whole = pltpu.make_async_remote_copy(
            src_ref=src.at[pl.ds(0, (nr - 1) * S)],
            dst_ref=dst.at[pl.ds(base(dst), (nr - 1) * S)],
            send_sem=sems.at[sem],
            recv_sem=sems.at[sem + 1],
            device_id=(g, lax.rem(r + 1, nr)),
            device_id_type=MESH,
        )
        whole.wait_send()
        whole.wait_recv()
        for side in range(2):
            one = group_copy(src, dst, sem, side)
            one.wait_send()
            one.wait_recv()

    start_all(send, tbl, 0)
    for load in loads[5:]:
        load.wait()

    count = jnp.full((1, P_SIZE), cnt[0], jnp.int32)
    ids = lax.broadcasted_iota(jnp.int32, (CD, P_SIZE), 0)

    def pack_ratios(out):
        def pack_one(j, carry):
            for s in range(S):
                out[j * S + s] = cown[pl.ds(rsend[0, s, j], 1), :]
            return carry

        def pack_side(j, carry):
            for side in range(2):
                out[nr * S + side * SG + j] = cown[pl.ds(gsend[0, side, j], 1), :]
            return carry

        lax.fori_loop(0, nr, pack_one, 0)
        lax.fori_loop(0, SG, pack_side, 0)

    stay = energy[...] / dens[...]
    for i in range(NA):
        stay = jnp.where((ids == act[0, i]) & (count > i), 0.0, stay)
    cown[...] = stay
    pack_ratios(csend0)
    start_all(csend0, ctbl0, 6)

    tbl[pl.ds(CD + r * S, S)] = send[pl.ds(r * S, S)]

    def fill(j, carry):
        at = pl.ds(j * 8, 8)
        tbl[at] = cells[at]
        return carry

    lax.fori_loop(0, CD // 8, fill, 0)
    origin = jnp.concatenate(
        [
            jnp.broadcast_to(jnp.sum(cells[0, 0:3, :], axis=1, keepdims=True) / P_SIZE, (3, P_SIZE)),
            jnp.zeros((1, P_SIZE), jnp.float32),
        ],
        axis=0,
    )

    def list_cells(i, carry):
        listed[i * NL] = act[0, i]
        for k in range(K):
            listed[i * NL + 1 + k] = nb[0, i, k]
        return carry

    lax.fori_loop(0, NA, list_cells, 0)
    one_row = jnp.ones((1, P_SIZE), jnp.float32)
    zero_rows = jnp.zeros((3, P_SIZE), jnp.float32)

    def partner_factors(cell):
        a, b, c = three_parts(
            jnp.concatenate([cell[0:3], square_length(cell), one_row, zero_rows], axis=0)
        )
        return jnp.concatenate([a, b, c, a, b, a], axis=0).astype(jnp.bfloat16)

    def own_factors(j, carry):
        for u in range(4):
            rhs[j * 4 + u] = partner_factors(cells[j * 4 + u] - origin)
        return carry

    lax.fori_loop(0, CD // 4, own_factors, 0)

    def own_rows(i, carry):
        at = act[0, i]
        cell = cells[at] - origin
        a, b, c = three_parts(
            jnp.concatenate([-2.0 * cell[0:3], one_row, square_length(cell), zero_rows], axis=0)
        )
        wide = jnp.concatenate(
            [a, a, a, b, b, c, jnp.zeros((P_SIZE - 48, P_SIZE), jnp.float32)], axis=0
        )
        lhs[i] = jnp.transpose(wide)[:, 0:48].astype(jnp.bfloat16)
        h = lanes_to_rows(smooth[pl.ds(at, 1), :])
        hbuf[0, i] = h
        hbuf[1, i] = 0.5 * (h * h * h)
        return carry

    lax.fori_loop(0, NA, own_rows, 0)

    def density_of(i, k, square, m):
        h = hbuf[0, i]
        square = jnp.maximum(square, tiny)
        inv = lax.rsqrt(square)
        d = square * inv
        t = jnp.maximum(h - d, 0.0)
        dbuf[i * NL + k] = d
        ibuf[i * NL + k] = inv
        return m * jnp.minimum(t * t * t, hbuf[1, i] - 3.0 * (square * t))

    def density_self(i, carry):
        at = act[0, i]
        square = jnp.dot(lhs[i], rhs[at], preferred_element_type=jnp.float32)
        part[i] = density_of(i, 0, square, cells[at][3:4])
        return carry

    lax.fori_loop(0, NA, density_self, 0)
    wait_all(send, tbl, 0)

    def other_factors(j, carry):
        for u in range(4):
            c = CD + j * 4 + u
            rhs[c] = partner_factors(tbl[c] - origin)
        return carry

    lax.fori_loop(0, (TB - CD) // 4, other_factors, 0)

    def density(i, carry):
        total = part[i]
        for k in range(1, NL, 2):
            first, second = nb[0, i, k - 1], nb[0, i, k]
            square = jnp.dot(
                lhs[i],
                jnp.concatenate([rhs[first], rhs[second]], axis=1),
                preferred_element_type=jnp.float32,
            )
            total += density_of(i, k, square[:, :P_SIZE], tbl[first][3:4])
            total += density_of(i, k + 1, square[:, P_SIZE:], tbl[second][3:4])
        part[i] = total
        return carry

    lax.fori_loop(0, NA, density, 0)

    fresh = dens[...]
    for i in range(NA):
        used = count > i
        h = smooth[pl.ds(act[0, i], 1), :]
        h3 = h * h * h
        rho = density_factor / (h3 * h3) * jnp.sum(jnp.transpose(part[i]), axis=0, keepdims=True)
        rho_out[i : i + 1, :] = jnp.where(used, rho, 0.0)
        fresh = jnp.where((ids == act[0, i]) & used, rho, fresh)
        rows[i : i + 1, :] = rho
        mine[i, 0:3, :] = cells[act[0, i]][0:3]
        mine[i, 3:4, :] = h
    cown[...] = energy[...] / fresh

    pack_ratios(csend)
    start_all(csend, ctbl, 12)

    ctbl[pl.ds(CD + r * S, S)] = csend[pl.ds(r * S, S)]
    ctbl[pl.ds(0, CD)] = jnp.zeros((CD, 1, P_SIZE), jnp.float32)

    def partner_weights(cell, ratio):
        base = cell[3:4] * jnp.concatenate([one_row, cell[0:3]], axis=0)
        a, b, c = three_parts(jnp.concatenate([base, base * ratio], axis=0))
        return jnp.concatenate([a, b, c, jnp.zeros_like(a)], axis=0).astype(jnp.bfloat16)

    def own_weights(j, carry):
        for u in range(4):
            c = j * 4 + u
            weights[c] = partner_weights(cells[c] - origin, cown[pl.ds(c, 1), :])
        return carry

    lax.fori_loop(0, CD // 4, own_weights, 0)
    wait_all(csend0, ctbl0, 6)
    ctbl0[pl.ds(r * S, S)] = csend[pl.ds(r * S, S)]

    def other_weights(j, carry):
        for u in range(4):
            c = j * 4 + u
            weights[CD + c] = partner_weights(tbl[CD + c] - origin, ctbl0[c])
        return carry

    lax.fori_loop(0, (TB - CD) // 4, other_weights, 0)
    known = jnp.concatenate(
        [ctbl0[...].reshape(TB - CD, P_SIZE), jnp.ones((2 * CD - TB, P_SIZE), jnp.float32)], axis=0
    )
    flags[...] = jnp.transpose(known)[0:1, :]

    def force(i, carry):
        h = hbuf[0, i]
        total = jnp.zeros((P_SIZE, 32), jnp.float32)
        for k in range(0, NL, 3):
            slopes, wide = [], []
            for at in range(k, k + 3):
                d = dbuf[i * NL + at]
                t = jnp.maximum(h - d, 0.0)
                value = jnp.where(t > d, t + t - d, t * t * ibuf[i * NL + at])
                a = value.astype(jnp.bfloat16)
                slopes += [a, (value - a.astype(jnp.float32)).astype(jnp.bfloat16)]
                wide += [weights[listed[i * NL + at]]] * 2
            total += lax.dot_general(
                jnp.concatenate(slopes, axis=1),
                jnp.concatenate(wide, axis=1),
                (((1,), (1,)), ((), ())),
                preferred_element_type=jnp.float32,
            )
        part[i, :, 0:32] = total
        return carry

    lax.fori_loop(0, NA, force, 0)

    for i in range(NA):
        used = count > i
        at = act[0, i]
        cell = cells[at] - origin
        h = smooth[pl.ds(at, 1), :]
        h3 = h * h * h
        scale = force_factor / (h3 * h3)
        ratio = energy[pl.ds(at, 1), :] / rows[i : i + 1, :]
        sums = jnp.transpose(part[i])
        sums = sums[0:8] + sums[8:16] + sums[16:24]
        for f in range(3):
            x = cell[f : f + 1]
            mine = x * sums[0:1] - sums[f + 1 : f + 2]
            theirs = x * sums[4:5] - sums[f + 5 : f + 6]
            acc_out[f : f + 1, i * P_SIZE : (i + 1) * P_SIZE] = jnp.where(
                used, scale * (ratio * mine + theirs), 0.0
            )

    wait_all(csend, ctbl, 12)


def late_terms(flags, cnt, nb, rho_in, acc_in, tbl, ctbl, mine, rho_out, acc_out, work):
    rho_out[...] = rho_in[...]
    acc_out[...] = acc_in[...]

    def find(i, found):
        for k in range(K):
            c = nb[0, i, k]
            hit = (c >= CD) & (flags[0, jnp.maximum(c - CD, 0)] == 0.0)
            work[found] = i * TB + c
            found += hit.astype(jnp.int32)
        return found

    found = lax.fori_loop(0, cnt[0], find, 0)

    def add(n, carry):
        i, c = lax.div(work[n], TB), lax.rem(work[n], TB)
        own, other = mine[i], tbl[c]
        h = own[3:4]
        strength = lanes_to_rows(other[3:4] * ctbl[c])
        diff = [own[f : f + 1] - lanes_to_rows(other[f : f + 1]) for f in range(3)]
        square = jnp.maximum(diff[0] * diff[0] + diff[1] * diff[1] + diff[2] * diff[2], tiny)
        inv = lax.rsqrt(square)
        d = square * inv
        t = jnp.maximum(h - d, 0.0)
        weight = strength * jnp.where(t > d, t + t - d, t * t * inv)
        h3 = h * h * h
        scale = force_factor / (h3 * h3)
        at = pl.ds(pl.multiple_of(i * P_SIZE, P_SIZE), P_SIZE)
        for f in range(3):
            acc_out[f : f + 1, at] += scale * jnp.sum(weight * diff[f], axis=0, keepdims=True)
        return carry

    lax.fori_loop(0, found, add, 0)


def body(pos, vel, mass, smooth, energy, dens, act, cnt, nb, rsend, gsend):
    ng, nr = lax.axis_size("group"), lax.axis_size("region")
    square = lambda v: v.reshape(CD, P_SIZE)
    hbm = pl.BlockSpec(memory_space=pltpu.HBM)
    vmem = pl.BlockSpec(memory_space=pltpu.VMEM)
    smem = pl.BlockSpec(memory_space=pltpu.SMEM)
    f32, b16 = jnp.float32, jnp.bfloat16
    args = (
        pos,
        vel,
        square(mass),
        square(smooth),
        square(energy),
        square(dens),
        act,
        cnt,
        nb,
        jnp.transpose(rsend, (0, 2, 1)),
        gsend,
    )
    args = tuple(pltpu.with_memory_space_constraint(v, pltpu.HBM) for v in args[:6]) + (
        (act, cnt) + tuple(pltpu.with_memory_space_constraint(v, pltpu.HBM) for v in args[8:])
    )
    held = [pltpu.VMEM(v.shape, f32) for v in args[:6]] + [pltpu.SMEM(v.shape, jnp.int32) for v in args[6:]]
    sent = nr * S + 2 * SG
    results = (
        jax.ShapeDtypeStruct((NA, P_SIZE), f32),
        jax.ShapeDtypeStruct((3, NA * P_SIZE), f32),
    )
    rho, acc, table, ratios, flags, mine, near = pl.pallas_call(
        functools.partial(kernel, ng, nr),
        out_shape=results
        + (
            jax.ShapeDtypeStruct((TB, 4, P_SIZE), f32),
            jax.ShapeDtypeStruct((TB, 1, P_SIZE), f32),
            jax.ShapeDtypeStruct((1, P_SIZE), f32),
            jax.ShapeDtypeStruct((NA, 4, P_SIZE), f32),
            jax.ShapeDtypeStruct((1, NA, K), jnp.int32),
        ),
        in_specs=[hbm] * len(args),
        out_specs=(vmem,) * 7,
        scratch_shapes=held
        + [
            pltpu.SMEM((NA * NL,), jnp.int32),
            pltpu.VMEM((CD, 4, P_SIZE), f32),
            pltpu.VMEM((sent, 4, P_SIZE), f32),
            pltpu.VMEM((sent, 1, P_SIZE), f32),
            pltpu.VMEM((sent, 1, P_SIZE), f32),
            pltpu.VMEM((sent, 1, P_SIZE), f32),
            pltpu.VMEM((CD, P_SIZE), f32),
            pltpu.VMEM((TB, 48, P_SIZE), b16),
            pltpu.VMEM((NA, P_SIZE, 48), b16),
            pltpu.VMEM((TB, 32, P_SIZE), b16),
            pltpu.VMEM((2, NA, P_SIZE, P_SIZE), f32),
            pltpu.VMEM((NA, P_SIZE, P_SIZE), f32),
            pltpu.VMEM((NA, P_SIZE), f32),
            pltpu.VMEM((NA * NL, P_SIZE, P_SIZE), f32),
            pltpu.VMEM((NA * NL, P_SIZE, P_SIZE), f32),
            pltpu.SemaphoreType.DMA((len(args) + 1,)),
            pltpu.SemaphoreType.DMA((18,)),
        ],
        compiler_params=pltpu.CompilerParams(
            collective_id=0, has_side_effects=True, vmem_limit_bytes=44 * 1024 * 1024
        ),
    )(*args)
    rho, acc = pl.pallas_call(
        late_terms,
        out_shape=results,
        in_specs=[smem] * 3 + [vmem] * 5,
        out_specs=(vmem, vmem),
        scratch_shapes=[pltpu.SMEM((NA * K + 1,), jnp.int32)],
        compiler_params=pltpu.CompilerParams(vmem_limit_bytes=16 * 1024 * 1024),
    )(flags, cnt, near, rho, acc, table, ratios, mine)
    return rho.reshape(-1), acc


def solution(mesh):
    both = ("group", "region")
    placed = (
        P(None, both),
        P(None, both),
        P(both),
        P(both),
        P(both),
        P(both),
        P(both, None),
        P(both),
        P(both, None, None),
        P(both, None, None),
        P(both, None, None),
    )
    return jax.shard_map(
        body,
        mesh=mesh,
        in_specs=placed,
        out_specs=(P(both), P(None, both)),
        check_vma=False,
    )
```

```python
import functools
import math

import jax
import jax.numpy as jnp
from jax import lax
from jax.experimental import pallas as pl
from jax.experimental.pallas import tpu as pltpu
from jax.sharding import PartitionSpec as P

P_SIZE = 128
K = 26
S = 2
SG = 8
CD = 128
NA = 8
TB = 208
NL = K + 1
MESH = pl.DeviceIdType.MESH

step_time = 0.1
density_factor = 16.0 / math.pi
force_factor = 32.0 / math.pi
tiny = 1e-30


def lanes_to_rows(row):
    return jnp.transpose(jnp.broadcast_to(row, (P_SIZE, P_SIZE)))


def three_parts(value):
    first = value.astype(jnp.bfloat16).astype(jnp.float32)
    rest = value - first
    second = rest.astype(jnp.bfloat16).astype(jnp.float32)
    return first, second, rest - second


def square_length(cell):
    sq = cell * cell
    return sq[0:1] + sq[1:2] + sq[2:3]


def kernel(
    ng,
    nr,
    pos_in,
    vel_in,
    mass_in,
    smooth_in,
    energy_in,
    dens_in,
    act_in,
    cnt_in,
    nb_in,
    rsend_in,
    gsend_in,
    rho_out,
    acc_out,
    tbl,
    ctbl,
    flags,
    mine,
    nb_out,
    pos,
    vel,
    mass,
    smooth,
    energy,
    dens,
    act,
    cnt,
    nb,
    rsend,
    gsend,
    listed,
    cells,
    send,
    ctbl0,
    csend0,
    csend,
    cown,
    rhs,
    lhs,
    weights,
    hbuf,
    part,
    rows,
    sums,
    tbuf,
    ibuf,
    in_sems,
    sems,
):
    g = lax.axis_index("group")
    r = lax.axis_index("region")
    up = lax.rem(g + 1, ng)
    down = lax.rem(g + ng - 1, ng)
    ny, nz = nr // 8, 8

    loads = [
        pltpu.make_async_copy(src, dst, in_sems.at[n])
        for n, (src, dst) in enumerate(
            (
                (pos_in, pos),
                (vel_in, vel),
                (mass_in, mass),
                (rsend_in, rsend),
                (gsend_in, gsend),
                (energy_in, energy),
                (dens_in, dens),
                (act_in, act),
                (cnt_in, cnt),
                (smooth_in, smooth),
                (nb_in, nb),
                (nb_in, nb_out),
            )
        )
    ]
    for load in loads[:5]:
        load.start()

    def far_to_near(k):
        a, b = lax.div(k, ny), lax.rem(k, ny)
        dz = nz // 2 + lax.div(a + 1, 2) * (1 - 2 * lax.rem(a, 2))
        dy = ny // 2 + lax.div(b + 1, 2) * (1 - 2 * lax.rem(b, 2))
        y, z = lax.div(r, nz), lax.rem(r, nz)
        return lax.rem(y + dy, ny) * nz + lax.rem(z + dz, nz)

    barrier = pltpu.get_barrier_semaphore()

    def greet(k, carry):
        pl.semaphore_signal(barrier, inc=1, device_id=(g, far_to_near(k)), device_id_type=MESH)
        return carry

    lax.fori_loop(0, nr - 1, greet, 0)
    pl.semaphore_signal(barrier, inc=1, device_id=(up, r), device_id_type=MESH)
    pl.semaphore_signal(barrier, inc=1, device_id=(down, r), device_id_type=MESH)

    for load in loads[5:]:
        load.start()

    def drifted(c):
        at = pl.ds(pl.multiple_of(c * P_SIZE, P_SIZE), P_SIZE)
        return pos[:, at] + step_time * vel[:, at]

    def gather(j, carry):
        for u in range(8):
            c = j * 8 + u
            cells[c, 0:3, :] = drifted(c)
            cells[c, 3:4, :] = mass[pl.ds(c, 1), :]
        return carry

    for load in loads[:5]:
        load.wait()
    lax.fori_loop(0, CD // 8, gather, 0)

    def pack_region(j, carry):
        for s in range(S):
            send[j * S + s] = cells[rsend[0, s, j]]
        return carry

    def pack_group(j, carry):
        for side in range(2):
            send[nr * S + side * SG + j] = cells[gsend[0, side, j]]
        return carry

    lax.fori_loop(0, nr, pack_region, 0)
    lax.fori_loop(0, SG, pack_group, 0)

    pl.semaphore_wait(barrier, nr + 1)

    def base(table):
        return table.shape[0] - nr * S - 2 * SG

    def region_copy(src, dst, sem, peer):
        return pltpu.make_async_remote_copy(
            src_ref=src.at[pl.ds(peer * S, S)],
            dst_ref=dst.at[pl.ds(base(dst) + r * S, S)],
            send_sem=sems.at[sem],
            recv_sem=sems.at[sem + 1],
            device_id=(g, peer),
            device_id_type=MESH,
        )

    def group_copy(src, dst, sem, side):
        return pltpu.make_async_remote_copy(
            src_ref=src.at[pl.ds(nr * S + side * SG, SG)],
            dst_ref=dst.at[pl.ds(base(dst) + nr * S + (1 - side) * SG, SG)],
            send_sem=sems.at[sem + 2 + 2 * side],
            recv_sem=sems.at[sem + 3 + 2 * side],
            device_id=(up if side else down, r),
            device_id_type=MESH,
        )

    def start_all(src, dst, sem):
        def go(k, carry):
            region_copy(src, dst, sem, far_to_near(k)).start()
            return carry

        lax.fori_loop(0, nr - 1, go, 0)
        group_copy(src, dst, sem, 0).start()
        group_copy(src, dst, sem, 1).start()

    def all_copies(src, dst, sem):
        whole = pltpu.make_async_remote_copy(
            src_ref=src.at[pl.ds(0, (nr - 1) * S)],
            dst_ref=dst.at[pl.ds(base(dst), (nr - 1) * S)],
            send_sem=sems.at[sem],
            recv_sem=sems.at[sem + 1],
            device_id=(g, lax.rem(r + 1, nr)),
            device_id_type=MESH,
        )
        return whole, group_copy(src, dst, sem, 0), group_copy(src, dst, sem, 1)

    def wait_all(src, dst, sem):
        for one in all_copies(src, dst, sem):
            one.wait_recv()

    start_all(send, tbl, 0)
    for load in loads[5:]:
        load.wait()

    count = jnp.full((1, P_SIZE), cnt[0], jnp.int32)
    ids = lax.broadcasted_iota(jnp.int32, (CD, P_SIZE), 0)

    def pack_ratios(out):
        def pack_one(j, carry):
            for s in range(S):
                out[j * S + s] = cown[pl.ds(rsend[0, s, j], 1), :]
            return carry

        def pack_side(j, carry):
            for side in range(2):
                out[nr * S + side * SG + j] = cown[pl.ds(gsend[0, side, j], 1), :]
            return carry

        lax.fori_loop(0, nr, pack_one, 0)
        lax.fori_loop(0, SG, pack_side, 0)

    stay = energy[...] / dens[...]
    for i in range(NA):
        stay = jnp.where((ids == act[0, i]) & (count > i), 0.0, stay)
    cown[...] = stay
    pack_ratios(csend0)

    tbl[pl.ds(CD + r * S, S)] = send[pl.ds(r * S, S)]

    def fill(j, carry):
        at = pl.ds(j * 8, 8)
        tbl[at] = cells[at]
        return carry

    lax.fori_loop(0, CD // 8, fill, 0)
    origin = jnp.concatenate(
        [
            jnp.broadcast_to(jnp.sum(cells[0, 0:3, :], axis=1, keepdims=True) / P_SIZE, (3, P_SIZE)),
            jnp.zeros((1, P_SIZE), jnp.float32),
        ],
        axis=0,
    )

    def list_cells(i, carry):
        listed[i * NL] = act[0, i]
        for k in range(K):
            listed[i * NL + 1 + k] = nb[0, i, k]
        return carry

    lax.fori_loop(0, NA, list_cells, 0)
    one_row = jnp.ones((1, P_SIZE), jnp.float32)
    zero_rows = jnp.zeros((3, P_SIZE), jnp.float32)

    def partner_factors(cell):
        a, b, c = three_parts(
            jnp.concatenate([cell[0:3], square_length(cell), one_row, zero_rows], axis=0)
        )
        return jnp.concatenate([a, b, c, a, b, a], axis=0).astype(jnp.bfloat16)

    def own_factors(j, carry):
        for u in range(4):
            rhs[j * 4 + u] = partner_factors(cells[j * 4 + u] - origin)
        return carry

    lax.fori_loop(0, CD // 4, own_factors, 0)

    def own_rows(i, carry):
        at = act[0, i]
        cell = cells[at] - origin
        a, b, c = three_parts(
            jnp.concatenate([-2.0 * cell[0:3], one_row, square_length(cell), zero_rows], axis=0)
        )
        wide = jnp.concatenate(
            [a, a, a, b, b, c, jnp.zeros((P_SIZE - 48, P_SIZE), jnp.float32)], axis=0
        )
        lhs[i] = jnp.transpose(wide)[:, 0:48].astype(jnp.bfloat16)
        h = lanes_to_rows(smooth[pl.ds(at, 1), :])
        hbuf[0, i] = h
        hbuf[1, i] = 0.5 * (h * h * h)
        return carry

    lax.fori_loop(0, NA, own_rows, 0)

    def density_of(i, k, square, m):
        h = hbuf[0, i]
        square = jnp.maximum(square, tiny)
        inv = lax.rsqrt(square)
        d = square * inv
        t = jnp.maximum(h - d, 0.0)
        tbuf[i * NL + k] = t
        ibuf[i * NL + k] = inv
        return m * jnp.minimum(t * t * t, hbuf[1, i] - 3.0 * (square * t))

    def density_self(i, carry):
        at = act[0, i]
        square = jnp.dot(lhs[i], rhs[at], preferred_element_type=jnp.float32)
        part[i] = density_of(i, 0, square, cells[at][3:4])
        return carry

    lax.fori_loop(0, NA, density_self, 0)
    wait_all(send, tbl, 0)

    def other_factors(j, carry):
        for u in range(4):
            c = CD + j * 4 + u
            rhs[c] = partner_factors(tbl[c] - origin)
        return carry

    lax.fori_loop(0, (TB - CD) // 4, other_factors, 0)

    def finish_density(i):
        sums[i, 0:1, :] = jnp.sum(jnp.transpose(part[i]), axis=0, keepdims=True)

    def start_ratio(k):
        region_copy(csend0, ctbl0, 6, far_to_near(k)).start()

    def more_ratios(k, carry):
        start_ratio(k)
        return carry

    lax.fori_loop(3 * NA, nr - 1, more_ratios, 0)
    group_copy(csend0, ctbl0, 6, 0).start()
    group_copy(csend0, ctbl0, 6, 1).start()

    def density(i, carry):
        for u in range(3):
            start_ratio(i * 3 + u)
        finish_density(lax.rem(i + NA - 1, NA))
        total = part[i]
        for k in range(1, NL, 2):
            first, second = nb[0, i, k - 1], nb[0, i, k]
            square = jnp.dot(
                lhs[i],
                jnp.concatenate([rhs[first], rhs[second]], axis=1),
                preferred_element_type=jnp.float32,
            )
            total += density_of(i, k, square[:, :P_SIZE], tbl[first][3:4])
            total += density_of(i, k + 1, square[:, P_SIZE:], tbl[second][3:4])
        part[i] = total
        return carry

    lax.fori_loop(0, NA, density, 0)
    finish_density(NA - 1)

    fresh = dens[...]
    for i in range(NA):
        used = count > i
        h = smooth[pl.ds(act[0, i], 1), :]
        h3 = h * h * h
        rho = density_factor / (h3 * h3) * sums[i, 0:1, :]
        rho_out[i : i + 1, :] = jnp.where(used, rho, 0.0)
        fresh = jnp.where((ids == act[0, i]) & used, rho, fresh)
        rows[i : i + 1, :] = rho
    cown[...] = energy[...] / fresh

    pack_ratios(csend)

    def partner_weights(cell, ratio):
        base = cell[3:4] * jnp.concatenate([one_row, cell[0:3]], axis=0)
        a, b, c = three_parts(jnp.concatenate([base, base * ratio], axis=0))
        return jnp.concatenate([a, b, c, jnp.zeros_like(a)], axis=0).astype(jnp.bfloat16)

    def own_weights(j):
        for u in range(CD // nr):
            c = j * (CD // nr) + u
            weights[c] = partner_weights(cells[c] - origin, cown[pl.ds(c, 1), :])

    def send_and_weigh(k, carry):
        region_copy(csend, ctbl, 12, far_to_near(k)).start()
        own_weights(k)
        return carry

    lax.fori_loop(0, nr - 1, send_and_weigh, 0)
    group_copy(csend, ctbl, 12, 0).start()
    group_copy(csend, ctbl, 12, 1).start()
    own_weights(nr - 1)
    ctbl[pl.ds(CD + r * S, S)] = csend[pl.ds(r * S, S)]
    for i in range(NA):
        mine[i, 0:3, :] = cells[act[0, i]][0:3]
        mine[i, 3:4, :] = smooth[pl.ds(act[0, i], 1), :]
    wait_all(csend0, ctbl0, 6)
    ctbl0[pl.ds(r * S, S)] = csend[pl.ds(r * S, S)]

    def other_weights(j, carry):
        for u in range(4):
            c = j * 4 + u
            weights[CD + c] = partner_weights(tbl[CD + c] - origin, ctbl0[c])
        return carry

    lax.fori_loop(0, (TB - CD) // 4, other_weights, 0)
    known = jnp.concatenate(
        [ctbl0[...].reshape(TB - CD, P_SIZE), jnp.ones((2 * CD - TB, P_SIZE), jnp.float32)], axis=0
    )
    flags[...] = jnp.transpose(known)[0:1, :]

    def finish_force(i):
        both = jnp.transpose(part[i])
        sums[i] = both[0:8] + both[8:16] + both[16:24]

    def force(i, carry):
        finish_force(lax.rem(i + NA - 1, NA))
        h = hbuf[0, i]
        total = jnp.zeros((P_SIZE, 32), jnp.float32)
        for k in range(0, NL, 3):
            slopes, wide = [], []
            for at in range(k, k + 3):
                t = tbuf[i * NL + at]
                twice = t + t
                value = jnp.where(twice > h, (twice + t) - h, t * (t * ibuf[i * NL + at]))
                a = value.astype(jnp.bfloat16)
                slopes += [a, (value - a.astype(jnp.float32)).astype(jnp.bfloat16)]
                wide += [weights[listed[i * NL + at]]] * 2
            total += lax.dot_general(
                jnp.concatenate(slopes, axis=1),
                jnp.concatenate(wide, axis=1),
                (((1,), (1,)), ((), ())),
                preferred_element_type=jnp.float32,
            )
        part[i, :, 0:32] = total
        return carry

    lax.fori_loop(0, NA, force, 0)
    finish_force(NA - 1)

    for i in range(NA):
        used = count > i
        at = act[0, i]
        cell = cells[at] - origin
        h = smooth[pl.ds(at, 1), :]
        h3 = h * h * h
        scale = force_factor / (h3 * h3)
        ratio = energy[pl.ds(at, 1), :] / rows[i : i + 1, :]
        for f in range(3):
            x = cell[f : f + 1]
            near = x * sums[i, 0:1, :] - sums[i, f + 1 : f + 2, :]
            far = x * sums[i, 4:5, :] - sums[i, f + 5 : f + 6, :]
            acc_out[f : f + 1, i * P_SIZE : (i + 1) * P_SIZE] = jnp.where(
                used, scale * (ratio * near + far), 0.0
            )

    wait_all(csend, ctbl, 12)
    for src, dst, sem in ((send, tbl, 0), (csend0, ctbl0, 6), (csend, ctbl, 12)):
        for one in all_copies(src, dst, sem):
            one.wait_send()


def late_terms(flags, cnt, nb, rho_in, acc_in, tbl, ctbl, mine, rho_out, acc_out, work):
    rho_out[...] = rho_in[...]
    acc_out[...] = acc_in[...]

    def find(i, found):
        for k in range(K):
            c = nb[0, i, k]
            hit = (c >= CD) & (flags[0, jnp.maximum(c - CD, 0)] == 0.0)
            work[found] = i * TB + c
            found += hit.astype(jnp.int32)
        return found

    found = lax.fori_loop(0, cnt[0], find, 0)

    def add(n, carry):
        i, c = lax.div(work[n], TB), lax.rem(work[n], TB)
        own, other = mine[i], tbl[c]
        h = own[3:4]
        strength = lanes_to_rows(other[3:4] * ctbl[c])
        diff = [own[f : f + 1] - lanes_to_rows(other[f : f + 1]) for f in range(3)]
        square = jnp.maximum(diff[0] * diff[0] + diff[1] * diff[1] + diff[2] * diff[2], tiny)
        inv = lax.rsqrt(square)
        d = square * inv
        t = jnp.maximum(h - d, 0.0)
        weight = strength * jnp.where(t > d, t + t - d, t * t * inv)
        h3 = h * h * h
        scale = force_factor / (h3 * h3)
        at = pl.ds(pl.multiple_of(i * P_SIZE, P_SIZE), P_SIZE)
        for f in range(3):
            acc_out[f : f + 1, at] += scale * jnp.sum(weight * diff[f], axis=0, keepdims=True)
        return carry

    lax.fori_loop(0, found, add, 0)


def body(pos, vel, mass, smooth, energy, dens, act, cnt, nb, rsend, gsend):
    ng, nr = lax.axis_size("group"), lax.axis_size("region")
    square = lambda v: v.reshape(CD, P_SIZE)
    hbm = pl.BlockSpec(memory_space=pltpu.HBM)
    vmem = pl.BlockSpec(memory_space=pltpu.VMEM)
    smem = pl.BlockSpec(memory_space=pltpu.SMEM)
    f32, b16 = jnp.float32, jnp.bfloat16
    args = (
        pos,
        vel,
        square(mass),
        square(smooth),
        square(energy),
        square(dens),
        act,
        cnt,
        nb,
        jnp.transpose(rsend, (0, 2, 1)),
        gsend,
    )
    pin = lambda v: pltpu.with_memory_space_constraint(v, pltpu.HBM)
    args = tuple(v if v is cnt else pin(v) for v in args)
    held = [pltpu.VMEM(v.shape, f32) for v in args[:6]] + [pltpu.SMEM(v.shape, jnp.int32) for v in args[6:]]
    sent = nr * S + 2 * SG
    results = (
        jax.ShapeDtypeStruct((NA, P_SIZE), f32),
        jax.ShapeDtypeStruct((3, NA * P_SIZE), f32),
    )
    rho, acc, table, ratios, flags, mine, near = pl.pallas_call(
        functools.partial(kernel, ng, nr),
        out_shape=results
        + (
            jax.ShapeDtypeStruct((TB, 4, P_SIZE), f32),
            jax.ShapeDtypeStruct((TB, 1, P_SIZE), f32),
            jax.ShapeDtypeStruct((1, P_SIZE), f32),
            jax.ShapeDtypeStruct((NA, 4, P_SIZE), f32),
            jax.ShapeDtypeStruct((1, NA, K), jnp.int32),
        ),
        in_specs=[hbm] * len(args),
        out_specs=(vmem,) * 7,
        scratch_shapes=held
        + [
            pltpu.SMEM((NA * NL,), jnp.int32),
            pltpu.VMEM((CD, 4, P_SIZE), f32),
            pltpu.VMEM((sent, 4, P_SIZE), f32),
            pltpu.VMEM((sent, 1, P_SIZE), f32),
            pltpu.VMEM((sent, 1, P_SIZE), f32),
            pltpu.VMEM((sent, 1, P_SIZE), f32),
            pltpu.VMEM((CD, P_SIZE), f32),
            pltpu.VMEM((TB, 48, P_SIZE), b16),
            pltpu.VMEM((NA, P_SIZE, 48), b16),
            pltpu.VMEM((TB, 32, P_SIZE), b16),
            pltpu.VMEM((2, NA, P_SIZE, P_SIZE), f32),
            pltpu.VMEM((NA, P_SIZE, P_SIZE), f32),
            pltpu.VMEM((NA, P_SIZE), f32),
            pltpu.VMEM((NA, 8, P_SIZE), f32),
            pltpu.VMEM((NA * NL, P_SIZE, P_SIZE), f32),
            pltpu.VMEM((NA * NL, P_SIZE, P_SIZE), f32),
            pltpu.SemaphoreType.DMA((len(args) + 1,)),
            pltpu.SemaphoreType.DMA((18,)),
        ],
        compiler_params=pltpu.CompilerParams(
            collective_id=0, has_side_effects=True, vmem_limit_bytes=44 * 1024 * 1024
        ),
    )(*args)
    rho, acc = pl.pallas_call(
        late_terms,
        out_shape=results,
        in_specs=[smem] * 3 + [vmem] * 5,
        out_specs=(vmem, vmem),
        scratch_shapes=[pltpu.SMEM((NA * K + 1,), jnp.int32)],
        compiler_params=pltpu.CompilerParams(vmem_limit_bytes=16 * 1024 * 1024),
    )(flags, cnt, near, rho, acc, table, ratios, mine)
    return rho.reshape(-1), acc


def solution(mesh):
    both = ("group", "region")
    placed = (
        P(None, both),
        P(None, both),
        P(both),
        P(both),
        P(both),
        P(both),
        P(both, None),
        P(both),
        P(both, None, None),
        P(both, None, None),
        P(both, None, None),
    )
    return jax.shard_map(
        body,
        mesh=mesh,
        in_specs=placed,
        out_specs=(P(both), P(None, both)),
        check_vma=False,
    )
```

```python
import functools
import math

import jax
import jax.numpy as jnp
from jax import lax
from jax.experimental import pallas as pl
from jax.experimental.pallas import tpu as pltpu
from jax.sharding import PartitionSpec as P

P_SIZE = 128
K = 26
S = 2
SG = 8
CD = 128
NA = 8
TB = 208
NL = K + 1
MESH = pl.DeviceIdType.MESH

step_time = 0.1
density_factor = 16.0 / math.pi
force_factor = 32.0 / math.pi
tiny = 1e-30


def lanes_to_rows(row):
    return jnp.transpose(jnp.broadcast_to(row, (P_SIZE, P_SIZE)))


def three_parts(value):
    first = value.astype(jnp.bfloat16).astype(jnp.float32)
    rest = value - first
    second = rest.astype(jnp.bfloat16).astype(jnp.float32)
    return first, second, rest - second


def square_length(cell):
    sq = cell * cell
    return sq[0:1] + sq[1:2] + sq[2:3]


def kernel(
    ng,
    nr,
    pos_in,
    vel_in,
    mass_in,
    smooth_in,
    energy_in,
    dens_in,
    act_in,
    cnt_in,
    nb_in,
    rsend_in,
    gsend_in,
    rho_out,
    acc_out,
    tbl,
    ctbl,
    flags,
    mine,
    nb_out,
    pos,
    vel,
    mass,
    smooth,
    energy,
    dens,
    act,
    cnt,
    nb,
    rsend,
    gsend,
    listed,
    remapped,
    cells,
    send,
    ctbl0,
    csend0,
    csend,
    cown,
    rhs,
    lhs,
    weights,
    hbuf,
    part,
    rows,
    sums,
    tbuf,
    qbuf,
    ibuf,
    in_sems,
    sems,
):
    g = lax.axis_index("group")
    r = lax.axis_index("region")
    up = lax.rem(g + 1, ng)
    down = lax.rem(g + ng - 1, ng)
    ny, nz = nr // 8, 8

    loads = [
        pltpu.make_async_copy(src, dst, in_sems.at[n])
        for n, (src, dst) in enumerate(
            (
                (pos_in, pos),
                (vel_in, vel),
                (mass_in, mass),
                (rsend_in, rsend),
                (gsend_in, gsend),
                (energy_in, energy),
                (dens_in, dens),
                (act_in, act),
                (cnt_in, cnt),
                (smooth_in, smooth),
                (nb_in, nb),
                (nb_in, nb_out),
            )
        )
    ]
    def far_to_near(k):
        a, b = lax.div(k, ny), lax.rem(k, ny)
        dz = nz // 2 + lax.div(a + 1, 2) * (1 - 2 * lax.rem(a, 2))
        dy = ny // 2 + lax.div(b + 1, 2) * (1 - 2 * lax.rem(b, 2))
        y, z = lax.div(r, nz), lax.rem(r, nz)
        return lax.rem(y + dy, ny) * nz + lax.rem(z + dz, nz)

    barrier = pltpu.get_barrier_semaphore()

    def greet(k, carry):
        pl.semaphore_signal(barrier, inc=1, device_id=(g, far_to_near(k)), device_id_type=MESH)
        return carry

    lax.fori_loop(0, nr - 1, greet, 0)
    pl.semaphore_signal(barrier, inc=1, device_id=(up, r), device_id_type=MESH)
    pl.semaphore_signal(barrier, inc=1, device_id=(down, r), device_id_type=MESH)

    for load in loads:
        load.start()

    def drifted(c):
        at = pl.ds(pl.multiple_of(c * P_SIZE, P_SIZE), P_SIZE)
        return pos[:, at] + step_time * vel[:, at]

    def gather(j, carry):
        for u in range(8):
            c = j * 8 + u
            cells[c, 0:3, :] = drifted(c)
            cells[c, 3:4, :] = mass[pl.ds(c, 1), :]
        return carry

    for load in loads[:5]:
        load.wait()
    lax.fori_loop(0, CD // 8, gather, 0)

    def pack_region(j, carry):
        for s in range(S):
            send[j * S + s] = cells[rsend[0, s, j]]
        return carry

    def pack_group(j, carry):
        for side in range(2):
            send[nr * S + side * SG + j] = cells[gsend[0, side, j]]
        return carry

    lax.fori_loop(0, nr, pack_region, 0)
    lax.fori_loop(0, SG, pack_group, 0)

    pl.semaphore_wait(barrier, nr + 1)

    def base(table):
        return table.shape[0] - nr * S - 2 * SG

    def region_copy(src, dst, sem, peer):
        return pltpu.make_async_remote_copy(
            src_ref=src.at[pl.ds(peer * S, S)],
            dst_ref=dst.at[pl.ds(base(dst) + r * S, S)],
            send_sem=sems.at[sem],
            recv_sem=sems.at[sem + 1],
            device_id=(g, peer),
            device_id_type=MESH,
        )

    def group_copy(src, dst, sem, side):
        return pltpu.make_async_remote_copy(
            src_ref=src.at[pl.ds(nr * S + side * SG, SG)],
            dst_ref=dst.at[pl.ds(base(dst) + nr * S + (1 - side) * SG, SG)],
            send_sem=sems.at[sem + 2 + 2 * side],
            recv_sem=sems.at[sem + 3 + 2 * side],
            device_id=(up if side else down, r),
            device_id_type=MESH,
        )

    def start_all(src, dst, sem):
        def go(k, carry):
            region_copy(src, dst, sem, far_to_near(k)).start()
            return carry

        lax.fori_loop(0, nr - 1, go, 0)
        group_copy(src, dst, sem, 0).start()
        group_copy(src, dst, sem, 1).start()

    def all_copies(src, dst, sem):
        whole = pltpu.make_async_remote_copy(
            src_ref=src.at[pl.ds(0, (nr - 1) * S)],
            dst_ref=dst.at[pl.ds(base(dst), (nr - 1) * S)],
            send_sem=sems.at[sem],
            recv_sem=sems.at[sem + 1],
            device_id=(g, lax.rem(r + 1, nr)),
            device_id_type=MESH,
        )
        return whole, group_copy(src, dst, sem, 0), group_copy(src, dst, sem, 1)

    def wait_all(src, dst, sem):
        for one in all_copies(src, dst, sem):
            one.wait_recv()

    start_all(send, tbl, 0)
    for load in loads[5:]:
        load.wait()

    count = jnp.full((1, P_SIZE), cnt[0], jnp.int32)
    ids = lax.broadcasted_iota(jnp.int32, (CD, P_SIZE), 0)

    def pack_ratios(out):
        def pack_one(j, carry):
            for s in range(S):
                out[j * S + s] = cown[pl.ds(rsend[0, s, j], 1), :]
            return carry

        def pack_side(j, carry):
            for side in range(2):
                out[nr * S + side * SG + j] = cown[pl.ds(gsend[0, side, j], 1), :]
            return carry

        lax.fori_loop(0, nr, pack_one, 0)
        lax.fori_loop(0, SG, pack_side, 0)

    stay = energy[...] / dens[...]
    for i in range(NA):
        stay = jnp.where((ids == act[0, i]) & (count > i), 0.0, stay)
    cown[...] = stay
    pack_ratios(csend0)
    start_all(csend0, ctbl0, 6)

    tbl[pl.ds(CD + r * S, S)] = send[pl.ds(r * S, S)]

    def fill(j, carry):
        at = pl.ds(j * 8, 8)
        tbl[at] = cells[at]
        return carry

    lax.fori_loop(0, CD // 8, fill, 0)
    origin = jnp.concatenate(
        [
            jnp.broadcast_to(jnp.sum(cells[0, 0:3, :], axis=1, keepdims=True) / P_SIZE, (3, P_SIZE)),
            jnp.zeros((1, P_SIZE), jnp.float32),
        ],
        axis=0,
    )

    remap = nb_out[0]
    spread = jnp.full((NA, K), cnt[0], jnp.int32)
    for i in range(NA):
        remap = jnp.where((remap == act[0, i]) & (spread > i), TB + i, remap)
    remapped[0] = remap
    to_scalar = pltpu.make_async_copy(remapped, listed, in_sems.at[len(loads)])
    to_scalar.start()

    one_row = jnp.ones((1, P_SIZE), jnp.float32)
    zero_rows = jnp.zeros((3, P_SIZE), jnp.float32)

    def partner_factors(cell):
        a, b, c = three_parts(
            jnp.concatenate([cell[0:3], square_length(cell), one_row, zero_rows], axis=0)
        )
        return jnp.concatenate([a, b, c, a, b, a], axis=0).astype(jnp.bfloat16)

    def partner_weights(cell, ratio):
        base = cell[3:4] * jnp.concatenate([one_row, cell[0:3]], axis=0)
        a, b, c = three_parts(jnp.concatenate([base, base * ratio], axis=0))
        return jnp.concatenate([a, b, c, jnp.zeros_like(a)], axis=0).astype(jnp.bfloat16)

    def own_factors(j, carry):
        for u in range(4):
            c = j * 4 + u
            cell = cells[c] - origin
            rhs[c] = partner_factors(cell)
            weights[c] = partner_weights(cell, cown[pl.ds(c, 1), :])
        return carry

    lax.fori_loop(0, CD // 4, own_factors, 0)

    def own_rows(i, carry):
        at = act[0, i]
        cell = cells[at] - origin
        a, b, c = three_parts(
            jnp.concatenate([-2.0 * cell[0:3], one_row, square_length(cell), zero_rows], axis=0)
        )
        wide = jnp.concatenate(
            [a, a, a, b, b, c, jnp.zeros((P_SIZE - 48, P_SIZE), jnp.float32)], axis=0
        )
        lhs[i] = jnp.transpose(wide)[:, 0:48].astype(jnp.bfloat16)
        h = lanes_to_rows(smooth[pl.ds(at, 1), :])
        hbuf[0, i] = h
        hbuf[1, i] = 0.5 * (h * h * h)
        hbuf[2, i] = 0.5 * h
        mine[i, 0:3, :] = cells[at][0:3]
        mine[i, 3:4, :] = smooth[pl.ds(at, 1), :]
        return carry

    lax.fori_loop(0, NA, own_rows, 0)

    def density_of(i, k, square, m):
        h = hbuf[0, i]
        square = jnp.maximum(square, tiny)
        inv = lax.rsqrt(square)
        d = square * inv
        t = jnp.maximum(h - d, 0.0)
        t2 = t * t
        tbuf[i * NL + k] = t
        qbuf[i * NL + k] = t2
        ibuf[i * NL + k] = inv
        return m * jnp.minimum(t2 * t, hbuf[1, i] - 3.0 * (square * t))

    def density_self(i, carry):
        at = act[0, i]
        square = jnp.dot(lhs[i], rhs[at], preferred_element_type=jnp.float32)
        part[i] = density_of(i, 0, square, cells[at][3:4])
        return carry

    lax.fori_loop(0, NA, density_self, 0)
    wait_all(send, tbl, 0)

    def other_factors(j, carry):
        for u in range(4):
            c = CD + j * 4 + u
            rhs[c] = partner_factors(tbl[c] - origin)
        return carry

    lax.fori_loop(0, (TB - CD) // 4, other_factors, 0)

    def finish_density(i):
        sums[i, 0:1, :] = jnp.sum(jnp.transpose(part[i]), axis=0, keepdims=True)

    def density(i, carry):
        finish_density(lax.rem(i + NA - 1, NA))
        total = part[i]
        for k in range(1, NL, 2):
            first, second = nb[0, i, k - 1], nb[0, i, k]
            square = jnp.dot(
                lhs[i],
                jnp.concatenate([rhs[first], rhs[second]], axis=1),
                preferred_element_type=jnp.float32,
            )
            total += density_of(i, k, square[:, :P_SIZE], tbl[first][3:4])
            total += density_of(i, k + 1, square[:, P_SIZE:], tbl[second][3:4])
        part[i] = total
        return carry

    lax.fori_loop(0, NA, density, 0)
    finish_density(NA - 1)

    fresh = dens[...]
    for i in range(NA):
        used = count > i
        h = smooth[pl.ds(act[0, i], 1), :]
        h3 = h * h * h
        rho = density_factor / (h3 * h3) * sums[i, 0:1, :]
        rho_out[i : i + 1, :] = jnp.where(used, rho, 0.0)
        fresh = jnp.where((ids == act[0, i]) & used, rho, fresh)
        rows[i : i + 1, :] = rho
    cown[...] = energy[...] / fresh

    pack_ratios(csend)

    wait_all(csend0, ctbl0, 6)
    ctbl0[pl.ds(r * S, S)] = csend[pl.ds(r * S, S)]

    def other_weights(c):
        weights[CD + c] = partner_weights(tbl[CD + c] - origin, ctbl0[c])

    def send_and_weigh(k, carry):
        region_copy(csend, ctbl, 12, far_to_near(k)).start()
        other_weights(2 * k)
        other_weights(2 * k + 1)
        return carry

    lax.fori_loop(0, nr - 1, send_and_weigh, 0)
    group_copy(csend, ctbl, 12, 0).start()
    group_copy(csend, ctbl, 12, 1).start()
    for c in range(2 * (nr - 1), TB - CD):
        other_weights(c)
    for i in range(NA):
        at = act[0, i]
        weights[TB + i] = partner_weights(
            cells[at] - origin, energy[pl.ds(at, 1), :] / rows[i : i + 1, :]
        )
    ctbl[pl.ds(CD + r * S, S)] = csend[pl.ds(r * S, S)]
    to_scalar.wait()
    known = jnp.concatenate(
        [ctbl0[...].reshape(TB - CD, P_SIZE), jnp.ones((2 * CD - TB, P_SIZE), jnp.float32)], axis=0
    )
    flags[...] = jnp.transpose(known)[0:1, :]

    def finish_force(i):
        both = jnp.transpose(part[i])
        sums[i] = both[0:8] + both[8:16] + both[16:24]

    def force(i, carry):
        finish_force(lax.rem(i + NA - 1, NA))
        h, half = hbuf[0, i], hbuf[2, i]
        total = jnp.zeros((P_SIZE, 32), jnp.float32)
        for k in range(0, NL, 3):
            slopes, wide = [], []
            for at in range(k, k + 3):
                t = tbuf[i * NL + at]
                value = jnp.where(t > half, 3.0 * t - h, qbuf[i * NL + at] * ibuf[i * NL + at])
                a = value.astype(jnp.bfloat16)
                slopes += [a, (value - a.astype(jnp.float32)).astype(jnp.bfloat16)]
                wide += [weights[listed[0, i, at - 1] if at else TB + i]] * 2
            total += lax.dot_general(
                jnp.concatenate(slopes, axis=1),
                jnp.concatenate(wide, axis=1),
                (((1,), (1,)), ((), ())),
                preferred_element_type=jnp.float32,
            )
        part[i, :, 0:32] = total
        return carry

    lax.fori_loop(0, NA, force, 0)
    finish_force(NA - 1)

    for i in range(NA):
        used = count > i
        at = act[0, i]
        cell = cells[at] - origin
        h = smooth[pl.ds(at, 1), :]
        h3 = h * h * h
        scale = force_factor / (h3 * h3)
        ratio = energy[pl.ds(at, 1), :] / rows[i : i + 1, :]
        for f in range(3):
            x = cell[f : f + 1]
            near = x * sums[i, 0:1, :] - sums[i, f + 1 : f + 2, :]
            far = x * sums[i, 4:5, :] - sums[i, f + 5 : f + 6, :]
            acc_out[f : f + 1, i * P_SIZE : (i + 1) * P_SIZE] = jnp.where(
                used, scale * (ratio * near + far), 0.0
            )

    wait_all(csend, ctbl, 12)
    for src, dst, sem in ((send, tbl, 0), (csend0, ctbl0, 6), (csend, ctbl, 12)):
        for one in all_copies(src, dst, sem):
            one.wait_send()


def late_terms(flags, cnt, nb, rho_in, acc_in, tbl, ctbl, mine, rho_out, acc_out, work):
    rho_out[...] = rho_in[...]
    acc_out[...] = acc_in[...]

    def find(i, found):
        for k in range(K):
            c = nb[0, i, k]
            hit = (c >= CD) & (flags[0, jnp.maximum(c - CD, 0)] == 0.0)
            work[found] = i * TB + c
            found += hit.astype(jnp.int32)
        return found

    found = lax.fori_loop(0, cnt[0], find, 0)

    def add(n, carry):
        i, c = lax.div(work[n], TB), lax.rem(work[n], TB)
        own, other = mine[i], tbl[c]
        h = own[3:4]
        strength = lanes_to_rows(other[3:4] * ctbl[c])
        diff = [own[f : f + 1] - lanes_to_rows(other[f : f + 1]) for f in range(3)]
        square = jnp.maximum(diff[0] * diff[0] + diff[1] * diff[1] + diff[2] * diff[2], tiny)
        inv = lax.rsqrt(square)
        d = square * inv
        t = jnp.maximum(h - d, 0.0)
        weight = strength * jnp.where(t > d, t + t - d, t * t * inv)
        h3 = h * h * h
        scale = force_factor / (h3 * h3)
        at = pl.ds(pl.multiple_of(i * P_SIZE, P_SIZE), P_SIZE)
        for f in range(3):
            acc_out[f : f + 1, at] += scale * jnp.sum(weight * diff[f], axis=0, keepdims=True)
        return carry

    lax.fori_loop(0, found, add, 0)


def body(pos, vel, mass, smooth, energy, dens, act, cnt, nb, rsend, gsend):
    ng, nr = lax.axis_size("group"), lax.axis_size("region")
    square = lambda v: v.reshape(CD, P_SIZE)
    hbm = pl.BlockSpec(memory_space=pltpu.HBM)
    vmem = pl.BlockSpec(memory_space=pltpu.VMEM)
    smem = pl.BlockSpec(memory_space=pltpu.SMEM)
    f32, b16 = jnp.float32, jnp.bfloat16
    args = (
        pos,
        vel,
        square(mass),
        square(smooth),
        square(energy),
        square(dens),
        act,
        cnt,
        nb,
        jnp.transpose(rsend, (0, 2, 1)),
        gsend,
    )
    pin = lambda v: pltpu.with_memory_space_constraint(v, pltpu.HBM)
    args = tuple(v if v is cnt else pin(v) for v in args)
    held = [pltpu.VMEM(v.shape, f32) for v in args[:6]] + [pltpu.SMEM(v.shape, jnp.int32) for v in args[6:]]
    sent = nr * S + 2 * SG
    results = (
        jax.ShapeDtypeStruct((NA, P_SIZE), f32),
        jax.ShapeDtypeStruct((3, NA * P_SIZE), f32),
    )
    rho, acc, table, ratios, flags, mine, near = pl.pallas_call(
        functools.partial(kernel, ng, nr),
        out_shape=results
        + (
            jax.ShapeDtypeStruct((TB, 4, P_SIZE), f32),
            jax.ShapeDtypeStruct((TB, 1, P_SIZE), f32),
            jax.ShapeDtypeStruct((1, P_SIZE), f32),
            jax.ShapeDtypeStruct((NA, 4, P_SIZE), f32),
            jax.ShapeDtypeStruct((1, NA, K), jnp.int32),
        ),
        in_specs=[hbm] * len(args),
        out_specs=(vmem,) * 7,
        scratch_shapes=held
        + [
            pltpu.SMEM((1, NA, K), jnp.int32),
            pltpu.VMEM((1, NA, K), jnp.int32),
            pltpu.VMEM((CD, 4, P_SIZE), f32),
            pltpu.VMEM((sent, 4, P_SIZE), f32),
            pltpu.VMEM((sent, 1, P_SIZE), f32),
            pltpu.VMEM((sent, 1, P_SIZE), f32),
            pltpu.VMEM((sent, 1, P_SIZE), f32),
            pltpu.VMEM((CD, P_SIZE), f32),
            pltpu.VMEM((TB, 48, P_SIZE), b16),
            pltpu.VMEM((NA, P_SIZE, 48), b16),
            pltpu.VMEM((TB + NA, 32, P_SIZE), b16),
            pltpu.VMEM((3, NA, P_SIZE, P_SIZE), f32),
            pltpu.VMEM((NA, P_SIZE, P_SIZE), f32),
            pltpu.VMEM((NA, P_SIZE), f32),
            pltpu.VMEM((NA, 8, P_SIZE), f32),
            pltpu.VMEM((NA * NL, P_SIZE, P_SIZE), f32),
            pltpu.VMEM((NA * NL, P_SIZE, P_SIZE), f32),
            pltpu.VMEM((NA * NL, P_SIZE, P_SIZE), f32),
            pltpu.SemaphoreType.DMA((len(args) + 2,)),
            pltpu.SemaphoreType.DMA((18,)),
        ],
        compiler_params=pltpu.CompilerParams(
            collective_id=0, has_side_effects=True, vmem_limit_bytes=50 * 1024 * 1024
        ),
    )(*args)
    rho, acc = pl.pallas_call(
        late_terms,
        out_shape=results,
        in_specs=[smem] * 3 + [vmem] * 5,
        out_specs=(vmem, vmem),
        scratch_shapes=[pltpu.SMEM((NA * K + 1,), jnp.int32)],
        compiler_params=pltpu.CompilerParams(vmem_limit_bytes=16 * 1024 * 1024),
    )(flags, cnt, near, rho, acc, table, ratios, mine)
    return rho.reshape(-1), acc


def solution(mesh):
    both = ("group", "region")
    placed = (
        P(None, both),
        P(None, both),
        P(both),
        P(both),
        P(both),
        P(both),
        P(both, None),
        P(both),
        P(both, None, None),
        P(both, None, None),
        P(both, None, None),
    )
    return jax.shard_map(
        body,
        mesh=mesh,
        in_specs=placed,
        out_specs=(P(both), P(None, both)),
        check_vma=False,
    )
```

```python
import functools
import math

import jax
import jax.numpy as jnp
from jax import lax
from jax.experimental import pallas as pl
from jax.experimental.pallas import tpu as pltpu
from jax.sharding import PartitionSpec as P

P_SIZE = 128
K = 26
S = 2
SG = 8
CD = 128
NA = 8
TB = 208
NL = K + 1
MESH = pl.DeviceIdType.MESH

step_time = 0.1
density_factor = 16.0 / math.pi
force_factor = 32.0 / math.pi
tiny = 1e-30


def lanes_to_rows(row):
    return jnp.transpose(jnp.broadcast_to(row, (P_SIZE, P_SIZE)))


def three_parts(value):
    first = value.astype(jnp.bfloat16).astype(jnp.float32)
    rest = value - first
    second = rest.astype(jnp.bfloat16).astype(jnp.float32)
    return first, second, rest - second


def square_length(cell):
    sq = cell * cell
    return sq[0:1] + sq[1:2] + sq[2:3]


def kernel(
    ng,
    nr,
    pos_in,
    vel_in,
    mass_in,
    smooth_in,
    energy_in,
    dens_in,
    act_in,
    cnt_in,
    nb_in,
    rsend_in,
    gsend_in,
    rho_out,
    acc_out,
    tbl,
    ctbl,
    mask_out,
    mine,
    nb_out,
    pos,
    vel,
    mass,
    smooth,
    energy,
    dens,
    act,
    cnt,
    nb,
    rsend,
    gsend,
    listed,
    remapped,
    flags,
    flag,
    masks,
    cells,
    send,
    ctbl0,
    csend0,
    csend,
    cown,
    rhs,
    lhs,
    weights,
    hbuf,
    part,
    rows,
    sums,
    tbuf,
    qbuf,
    ibuf,
    in_sems,
    sems,
):
    g = lax.axis_index("group")
    r = lax.axis_index("region")
    up = lax.rem(g + 1, ng)
    down = lax.rem(g + ng - 1, ng)
    ny, nz = nr // 8, 8

    loads = [
        pltpu.make_async_copy(src, dst, in_sems.at[n])
        for n, (src, dst) in enumerate(
            (
                (pos_in, pos),
                (vel_in, vel),
                (mass_in, mass),
                (rsend_in, rsend),
                (gsend_in, gsend),
                (energy_in, energy),
                (dens_in, dens),
                (act_in, act),
                (cnt_in, cnt),
                (smooth_in, smooth),
                (nb_in, nb),
                (nb_in, nb_out),
            )
        )
    ]
    def far_to_near(k):
        a, b = lax.div(k, ny), lax.rem(k, ny)
        dz = nz // 2 + lax.div(a + 1, 2) * (1 - 2 * lax.rem(a, 2))
        dy = ny // 2 + lax.div(b + 1, 2) * (1 - 2 * lax.rem(b, 2))
        y, z = lax.div(r, nz), lax.rem(r, nz)
        return lax.rem(y + dy, ny) * nz + lax.rem(z + dz, nz)

    barrier = pltpu.get_barrier_semaphore()

    def greet(k, carry):
        pl.semaphore_signal(barrier, inc=1, device_id=(g, far_to_near(k)), device_id_type=MESH)
        return carry

    lax.fori_loop(0, nr - 1, greet, 0)
    pl.semaphore_signal(barrier, inc=1, device_id=(up, r), device_id_type=MESH)
    pl.semaphore_signal(barrier, inc=1, device_id=(down, r), device_id_type=MESH)

    for load in loads:
        load.start()

    def drifted(c):
        at = pl.ds(pl.multiple_of(c * P_SIZE, P_SIZE), P_SIZE)
        return pos[:, at] + step_time * vel[:, at]

    def gather(j, carry):
        for u in range(8):
            c = j * 8 + u
            cells[c, 0:3, :] = drifted(c)
            cells[c, 3:4, :] = mass[pl.ds(c, 1), :]
        return carry

    for load in loads[:5]:
        load.wait()
    lax.fori_loop(0, CD // 8, gather, 0)

    def pack_region(j, carry):
        for u in range(8):
            for s in range(S):
                send[(j * 8 + u) * S + s] = cells[rsend[0, s, j * 8 + u]]
        return carry

    lax.fori_loop(0, nr // 8, pack_region, 0)
    for side in range(2):
        for j in range(SG):
            send[nr * S + side * SG + j] = cells[gsend[0, side, j]]

    pl.semaphore_wait(barrier, nr + 1)

    def base(table):
        return table.shape[0] - nr * S - 2 * SG

    def region_copy(src, dst, sem, peer):
        return pltpu.make_async_remote_copy(
            src_ref=src.at[pl.ds(peer * S, S)],
            dst_ref=dst.at[pl.ds(base(dst) + r * S, S)],
            send_sem=sems.at[sem],
            recv_sem=sems.at[sem + 1],
            device_id=(g, peer),
            device_id_type=MESH,
        )

    def group_copy(src, dst, sem, side):
        return pltpu.make_async_remote_copy(
            src_ref=src.at[pl.ds(nr * S + side * SG, SG)],
            dst_ref=dst.at[pl.ds(base(dst) + nr * S + (1 - side) * SG, SG)],
            send_sem=sems.at[sem + 2 + 2 * side],
            recv_sem=sems.at[sem + 3 + 2 * side],
            device_id=(up if side else down, r),
            device_id_type=MESH,
        )

    def start_all(src, dst, sem):
        def go(k, carry):
            region_copy(src, dst, sem, far_to_near(k)).start()
            return carry

        lax.fori_loop(0, nr - 1, go, 0)
        group_copy(src, dst, sem, 0).start()
        group_copy(src, dst, sem, 1).start()

    def all_copies(src, dst, sem):
        whole = pltpu.make_async_remote_copy(
            src_ref=src.at[pl.ds(0, (nr - 1) * S)],
            dst_ref=dst.at[pl.ds(base(dst), (nr - 1) * S)],
            send_sem=sems.at[sem],
            recv_sem=sems.at[sem + 1],
            device_id=(g, lax.rem(r + 1, nr)),
            device_id_type=MESH,
        )
        return whole, group_copy(src, dst, sem, 0), group_copy(src, dst, sem, 1)

    def wait_all(src, dst, sem):
        for one in all_copies(src, dst, sem):
            one.wait_recv()

    start_all(send, tbl, 0)
    for load in loads[5:]:
        load.wait()

    count = jnp.full((1, P_SIZE), cnt[0], jnp.int32)
    ids = lax.broadcasted_iota(jnp.int32, (CD, P_SIZE), 0)

    def pack_ratios(out):
        def pack_one(j, carry):
            for u in range(8):
                for s in range(S):
                    at = rsend[0, s, j * 8 + u]
                    out[(j * 8 + u) * S + s] = cown[pl.ds(at, 1), :]
            return carry

        lax.fori_loop(0, nr // 8, pack_one, 0)
        for side in range(2):
            for j in range(SG):
                out[nr * S + side * SG + j] = cown[pl.ds(gsend[0, side, j], 1), :]

    stay = energy[...] / dens[...]
    for i in range(NA):
        stay = jnp.where((ids == act[0, i]) & (count > i), 0.0, stay)
    cown[...] = stay
    pack_ratios(csend0)
    start_all(csend0, ctbl0, 6)

    tbl[pl.ds(CD + r * S, S)] = send[pl.ds(r * S, S)]

    def fill(j, carry):
        at = pl.ds(j * 8, 8)
        tbl[at] = cells[at]
        return carry

    lax.fori_loop(0, CD // 8, fill, 0)
    origin = jnp.concatenate(
        [
            jnp.broadcast_to(jnp.sum(cells[0, 0:3, :], axis=1, keepdims=True) / P_SIZE, (3, P_SIZE)),
            jnp.zeros((1, P_SIZE), jnp.float32),
        ],
        axis=0,
    )

    remap = nb_out[0]
    spread = jnp.full((NA, K), cnt[0], jnp.int32)
    for i in range(NA):
        remap = jnp.where((remap == act[0, i]) & (spread > i), TB + i, remap)
    remapped[0] = remap
    to_scalar = pltpu.make_async_copy(remapped, listed, in_sems.at[len(loads)])
    to_scalar.start()

    one_row = jnp.ones((1, P_SIZE), jnp.float32)
    zero_rows = jnp.zeros((3, P_SIZE), jnp.float32)

    def partner_factors(cell):
        a, b, c = three_parts(
            jnp.concatenate([cell[0:3], square_length(cell), one_row, zero_rows], axis=0)
        )
        return jnp.concatenate([a, b, c, a, b, a], axis=0).astype(jnp.bfloat16)

    def partner_weights(cell, ratio):
        base = cell[3:4] * jnp.concatenate([one_row, cell[0:3]], axis=0)
        a, b, c = three_parts(jnp.concatenate([base, base * ratio], axis=0))
        return jnp.concatenate([a, b, c, jnp.zeros_like(a)], axis=0).astype(jnp.bfloat16)

    def own_factors(j, carry):
        for u in range(4):
            c = j * 4 + u
            cell = cells[c] - origin
            rhs[c] = partner_factors(cell)
            weights[c] = partner_weights(cell, cown[pl.ds(c, 1), :])
        return carry

    lax.fori_loop(0, CD // 4, own_factors, 0)

    def own_rows(i, carry):
        at = act[0, i]
        cell = cells[at] - origin
        a, b, c = three_parts(
            jnp.concatenate([-2.0 * cell[0:3], one_row, square_length(cell), zero_rows], axis=0)
        )
        wide = jnp.concatenate(
            [a, a, a, b, b, c, jnp.zeros((P_SIZE - 48, P_SIZE), jnp.float32)], axis=0
        )
        lhs[i] = jnp.transpose(wide)[:, 0:48].astype(jnp.bfloat16)
        h = lanes_to_rows(smooth[pl.ds(at, 1), :])
        hbuf[0, i] = h
        hbuf[1, i] = 0.5 * (h * h * h)
        hbuf[2, i] = 0.5 * h
        width = smooth[pl.ds(at, 1), :]
        cube = width * width * width
        rows[0, pl.ds(i, 1), :] = 1.0 / (cube * cube)
        rows[1, pl.ds(i, 1), :] = energy[pl.ds(at, 1), :]
        for f in range(3):
            rows[2 + f, pl.ds(i, 1), :] = cell[f : f + 1]
        mine[i, 0:3, :] = cells[at][0:3]
        mine[i, 3:4, :] = smooth[pl.ds(at, 1), :]
        return carry

    lax.fori_loop(0, NA, own_rows, 0)

    def density_of(i, k, square, m):
        h = hbuf[0, i]
        square = jnp.maximum(square, tiny)
        inv = lax.rsqrt(square)
        d = square * inv
        t = jnp.maximum(h - d, 0.0)
        t2 = t * t
        tbuf[i * NL + k] = t
        qbuf[i * NL + k] = t2
        ibuf[i * NL + k] = inv
        return m * jnp.minimum(t2 * t, hbuf[1, i] - 3.0 * (square * t))

    def density_self(i, carry):
        at = act[0, i]
        square = jnp.dot(lhs[i], rhs[at], preferred_element_type=jnp.float32)
        part[i] = density_of(i, 0, square, cells[at][3:4])
        return carry

    lax.fori_loop(0, NA, density_self, 0)
    wait_all(send, tbl, 0)

    def other_factors(j, carry):
        for u in range(4):
            c = CD + j * 4 + u
            rhs[c] = partner_factors(tbl[c] - origin)
        return carry

    lax.fori_loop(0, (TB - CD) // 4, other_factors, 0)

    def finish_density(i):
        sums[0, pl.ds(i, 1), :] = jnp.sum(jnp.transpose(part[i]), axis=0, keepdims=True)

    def density(i, carry):
        finish_density(lax.rem(i + NA - 1, NA))
        total = part[i]
        for k in range(1, NL, 2):
            first, second = nb[0, i, k - 1], nb[0, i, k]
            square = jnp.dot(
                lhs[i],
                jnp.concatenate([rhs[first], rhs[second]], axis=1),
                preferred_element_type=jnp.float32,
            )
            total += density_of(i, k, square[:, :P_SIZE], tbl[first][3:4])
            total += density_of(i, k + 1, square[:, P_SIZE:], tbl[second][3:4])
        part[i] = total
        return carry

    lax.fori_loop(0, NA, density, 0)
    finish_density(NA - 1)

    slots = lax.broadcasted_iota(jnp.int32, (NA, P_SIZE), 0)
    in_use = slots < count
    rho = density_factor * rows[0] * sums[0]
    rho_out[...] = jnp.where(in_use, rho, 0.0)
    ratio = rows[1] / rho
    rows[5] = ratio
    fresh = stay
    for i in range(NA):
        fresh = jnp.where((ids == act[0, i]) & (count > i), ratio[i : i + 1], fresh)
    cown[...] = fresh
    pack_ratios(csend)

    wait_all(csend0, ctbl0, 6)
    ctbl0[pl.ds(r * S, S)] = csend[pl.ds(r * S, S)]
    known = jnp.concatenate(
        [ctbl0[...].reshape(TB - CD, P_SIZE), jnp.ones((2 * CD - TB, P_SIZE), jnp.float32)], axis=0
    )
    missing = (jnp.transpose(known)[0:1, :] == 0.0).astype(jnp.int32)
    flags[...] = jnp.concatenate([jnp.zeros((1, P_SIZE), jnp.int32), missing], axis=1)
    to_flags = pltpu.make_async_copy(flags, flag, in_sems.at[len(loads) + 1])
    to_flags.start()

    def other_weights(c):
        weights[CD + c] = partner_weights(tbl[CD + c] - origin, ctbl0[c])

    def send_and_weigh(k, carry):
        region_copy(csend, ctbl, 12, far_to_near(k)).start()
        other_weights(2 * k)
        other_weights(2 * k + 1)
        return carry

    lax.fori_loop(0, nr - 1, send_and_weigh, 0)
    group_copy(csend, ctbl, 12, 0).start()
    group_copy(csend, ctbl, 12, 1).start()
    for c in range(2 * (nr - 1), TB - CD):
        other_weights(c)
    for i in range(NA):
        at = act[0, i]
        weights[TB + i] = partner_weights(cells[at] - origin, rows[5, i : i + 1, :])
    ctbl[pl.ds(CD + r * S, S)] = csend[pl.ds(r * S, S)]
    to_scalar.wait()
    to_flags.wait()
    def finish_force(i):
        both = jnp.transpose(part[i])
        both = both[0:8] + both[8:16] + both[16:24]
        for f in range(8):
            sums[f, pl.ds(i, 1), :] = both[f : f + 1]

    def force(i, carry):
        finish_force(lax.rem(i + NA - 1, NA))
        h, half = hbuf[0, i], hbuf[2, i]
        total = jnp.zeros((P_SIZE, 32), jnp.float32)
        for k in range(0, NL, 3):
            slopes, wide = [], []
            for at in range(k, k + 3):
                t = tbuf[i * NL + at]
                value = jnp.where(t > half, 3.0 * t - h, qbuf[i * NL + at] * ibuf[i * NL + at])
                a = value.astype(jnp.bfloat16)
                slopes += [a, (value - a.astype(jnp.float32)).astype(jnp.bfloat16)]
                wide += [weights[listed[0, i, at - 1] if at else TB + i]] * 2
            total += lax.dot_general(
                jnp.concatenate(slopes, axis=1),
                jnp.concatenate(wide, axis=1),
                (((1,), (1,)), ((), ())),
                preferred_element_type=jnp.float32,
            )
        part[i, :, 0:32] = total
        hits = 0
        for k in range(K):
            hits += flag[0, listed[0, i, k]] * (1 << k)
        masks[0, i] = hits * jnp.minimum(jnp.maximum(cnt[0] - i, 0), 1)
        return carry

    lax.fori_loop(0, NA, force, 0)
    finish_force(NA - 1)
    to_masks = pltpu.make_async_copy(masks, mask_out, in_sems.at[len(loads) + 2])
    to_masks.start()

    for f in range(3):
        x = rows[2 + f]
        near = x * sums[0] - sums[f + 1]
        far = x * sums[4] - sums[f + 5]
        total = jnp.where(in_use, force_factor * rows[0] * (rows[5] * near + far), 0.0)
        for i in range(NA):
            acc_out[f : f + 1, i * P_SIZE : (i + 1) * P_SIZE] = total[i : i + 1]

    to_masks.wait()
    wait_all(csend, ctbl, 12)
    for src, dst, sem in ((send, tbl, 0), (csend0, ctbl0, 6), (csend, ctbl, 12)):
        for one in all_copies(src, dst, sem):
            one.wait_send()


def late_terms(masks, nb, rho_in, acc_in, tbl, ctbl, mine, rho_out, acc_out):
    rho_out[...] = rho_in[...]
    acc_out[...] = acc_in[...]

    def add(i, c):
        own, other = mine[i], tbl[c]
        h = own[3:4]
        strength = lanes_to_rows(other[3:4] * ctbl[c])
        diff = [own[f : f + 1] - lanes_to_rows(other[f : f + 1]) for f in range(3)]
        square = jnp.maximum(diff[0] * diff[0] + diff[1] * diff[1] + diff[2] * diff[2], tiny)
        inv = lax.rsqrt(square)
        d = square * inv
        t = jnp.maximum(h - d, 0.0)
        weight = strength * jnp.where(t > d, t + t - d, t * t * inv)
        h3 = h * h * h
        scale = force_factor / (h3 * h3)
        at = pl.ds(pl.multiple_of(i * P_SIZE, P_SIZE), P_SIZE)
        for f in range(3):
            acc_out[f : f + 1, at] += scale * jnp.sum(weight * diff[f], axis=0, keepdims=True)

    def slot(i, carry):
        def highest(left):
            k = 31 - lax.clz(left)
            add(i, nb[0, i, k])
            return left - lax.shift_left(1, k)

        lax.while_loop(lambda left: left != 0, highest, masks[0, i])
        return carry

    lax.fori_loop(0, NA, slot, 0)


def body(pos, vel, mass, smooth, energy, dens, act, cnt, nb, rsend, gsend):
    ng, nr = lax.axis_size("group"), lax.axis_size("region")
    square = lambda v: v.reshape(CD, P_SIZE)
    hbm = pl.BlockSpec(memory_space=pltpu.HBM)
    vmem = pl.BlockSpec(memory_space=pltpu.VMEM)
    smem = pl.BlockSpec(memory_space=pltpu.SMEM)
    f32, b16 = jnp.float32, jnp.bfloat16
    args = (
        pos,
        vel,
        square(mass),
        square(smooth),
        square(energy),
        square(dens),
        act,
        cnt,
        nb,
        jnp.transpose(rsend, (0, 2, 1)),
        gsend,
    )
    pin = lambda v: pltpu.with_memory_space_constraint(v, pltpu.HBM)
    args = tuple(v if v is cnt else pin(v) for v in args)
    held = [pltpu.VMEM(v.shape, f32) for v in args[:6]] + [pltpu.SMEM(v.shape, jnp.int32) for v in args[6:]]
    sent = nr * S + 2 * SG
    results = (
        jax.ShapeDtypeStruct((NA, P_SIZE), f32),
        jax.ShapeDtypeStruct((3, NA * P_SIZE), f32),
    )
    rho, acc, table, ratios, masks, mine, near = pl.pallas_call(
        functools.partial(kernel, ng, nr),
        out_shape=results
        + (
            jax.ShapeDtypeStruct((TB, 4, P_SIZE), f32),
            jax.ShapeDtypeStruct((TB, 1, P_SIZE), f32),
            jax.ShapeDtypeStruct((1, NA), jnp.int32),
            jax.ShapeDtypeStruct((NA, 4, P_SIZE), f32),
            jax.ShapeDtypeStruct((1, NA, K), jnp.int32),
        ),
        in_specs=[hbm] * len(args),
        out_specs=(vmem,) * 7,
        scratch_shapes=held
        + [
            pltpu.SMEM((1, NA, K), jnp.int32),
            pltpu.VMEM((1, NA, K), jnp.int32),
            pltpu.VMEM((1, 2 * P_SIZE), jnp.int32),
            pltpu.SMEM((1, 2 * P_SIZE), jnp.int32),
            pltpu.SMEM((1, NA), jnp.int32),
            pltpu.VMEM((CD, 4, P_SIZE), f32),
            pltpu.VMEM((sent, 4, P_SIZE), f32),
            pltpu.VMEM((sent, 1, P_SIZE), f32),
            pltpu.VMEM((sent, 1, P_SIZE), f32),
            pltpu.VMEM((sent, 1, P_SIZE), f32),
            pltpu.VMEM((CD, P_SIZE), f32),
            pltpu.VMEM((TB, 48, P_SIZE), b16),
            pltpu.VMEM((NA, P_SIZE, 48), b16),
            pltpu.VMEM((TB + NA, 32, P_SIZE), b16),
            pltpu.VMEM((3, NA, P_SIZE, P_SIZE), f32),
            pltpu.VMEM((NA, P_SIZE, P_SIZE), f32),
            pltpu.VMEM((6, NA, P_SIZE), f32),
            pltpu.VMEM((8, NA, P_SIZE), f32),
            pltpu.VMEM((NA * NL, P_SIZE, P_SIZE), f32),
            pltpu.VMEM((NA * NL, P_SIZE, P_SIZE), f32),
            pltpu.VMEM((NA * NL, P_SIZE, P_SIZE), f32),
            pltpu.SemaphoreType.DMA((len(args) + 4,)),
            pltpu.SemaphoreType.DMA((18,)),
        ],
        compiler_params=pltpu.CompilerParams(
            collective_id=0, has_side_effects=True, vmem_limit_bytes=50 * 1024 * 1024
        ),
    )(*args)
    rho, acc = pl.pallas_call(
        late_terms,
        out_shape=results,
        in_specs=[smem] * 2 + [vmem] * 5,
        out_specs=(vmem, vmem),
        compiler_params=pltpu.CompilerParams(vmem_limit_bytes=16 * 1024 * 1024),
    )(masks, near, rho, acc, table, ratios, mine)
    return rho.reshape(-1), acc


def solution(mesh):
    both = ("group", "region")
    placed = (
        P(None, both),
        P(None, both),
        P(both),
        P(both),
        P(both),
        P(both),
        P(both, None),
        P(both),
        P(both, None, None),
        P(both, None, None),
        P(both, None, None),
    )
    return jax.shard_map(
        body,
        mesh=mesh,
        in_specs=placed,
        out_specs=(P(both), P(None, both)),
        check_vma=False,
    )
```

```python
import functools
import math

import jax
import jax.numpy as jnp
from jax import lax
from jax.experimental import pallas as pl
from jax.experimental.pallas import tpu as pltpu
from jax.sharding import PartitionSpec as P

P_SIZE = 128
K = 26
S = 2
SG = 8
CD = 128
NA = 8
TB = 208
NL = K + 1
MESH = pl.DeviceIdType.MESH

step_time = 0.1
density_factor = 16.0 / math.pi
force_factor = 32.0 / math.pi
tiny = 1e-30


def lanes_to_rows(row):
    return jnp.transpose(jnp.broadcast_to(row, (P_SIZE, P_SIZE)))


def three_parts(value):
    first = value.astype(jnp.bfloat16).astype(jnp.float32)
    rest = value - first
    second = rest.astype(jnp.bfloat16).astype(jnp.float32)
    return first, second, rest - second


def square_length(cell):
    sq = cell * cell
    return sq[0:1] + sq[1:2] + sq[2:3]


def kernel(
    ng,
    nr,
    pos_in,
    vel_in,
    mass_in,
    smooth_in,
    energy_in,
    dens_in,
    act_in,
    cnt_in,
    nb_in,
    rsend_in,
    gsend_in,
    rho_out,
    acc_out,
    tbl,
    ctbl,
    mask_out,
    mine,
    nb_out,
    pos,
    vel,
    mass,
    smooth,
    energy,
    dens,
    act,
    cnt,
    nb,
    rsend,
    gsend,
    listed,
    remapped,
    flags,
    flag,
    masks,
    cells,
    send,
    ctbl0,
    csend0,
    csend,
    cown,
    rhs,
    lhs,
    weights,
    hbuf,
    part,
    rows,
    sums,
    tbuf,
    qbuf,
    ibuf,
    in_sems,
    sems,
):
    g = lax.axis_index("group")
    r = lax.axis_index("region")
    up = lax.rem(g + 1, ng)
    down = lax.rem(g + ng - 1, ng)
    ny, nz = nr // 8, 8

    loads = [
        pltpu.make_async_copy(src, dst, in_sems.at[n])
        for n, (src, dst) in enumerate(
            (
                (pos_in, pos),
                (vel_in, vel),
                (mass_in, mass),
                (rsend_in, rsend),
                (gsend_in, gsend),
                (energy_in, energy),
                (dens_in, dens),
                (act_in, act),
                (cnt_in, cnt),
                (smooth_in, smooth),
                (nb_in, nb),
                (nb_in, nb_out),
            )
        )
    ]
    def far_to_near(k):
        a, b = lax.div(k, ny), lax.rem(k, ny)
        dz = nz // 2 + lax.div(a + 1, 2) * (1 - 2 * lax.rem(a, 2))
        dy = ny // 2 + lax.div(b + 1, 2) * (1 - 2 * lax.rem(b, 2))
        y, z = lax.div(r, nz), lax.rem(r, nz)
        return lax.rem(y + dy, ny) * nz + lax.rem(z + dz, nz)

    for load in loads:
        load.start()

    barrier = pltpu.get_barrier_semaphore()

    def greet(k, carry):
        pl.semaphore_signal(barrier, inc=1, device_id=(g, far_to_near(k)), device_id_type=MESH)
        return carry

    lax.fori_loop(0, nr - 1, greet, 0)
    pl.semaphore_signal(barrier, inc=1, device_id=(up, r), device_id_type=MESH)
    pl.semaphore_signal(barrier, inc=1, device_id=(down, r), device_id_type=MESH)

    def drifted(c):
        at = pl.ds(pl.multiple_of(c * P_SIZE, P_SIZE), P_SIZE)
        return pos[:, at] + step_time * vel[:, at]

    def gather(j, carry):
        for u in range(8):
            c = j * 8 + u
            cells[c, 0:3, :] = drifted(c)
            cells[c, 3:4, :] = mass[pl.ds(c, 1), :]
        return carry

    for load in loads[:5]:
        load.wait()
    lax.fori_loop(0, CD // 8, gather, 0)

    def pack_region(j, carry):
        for u in range(8):
            for s in range(S):
                send[(j * 8 + u) * S + s] = cells[rsend[0, s, j * 8 + u]]
        return carry

    lax.fori_loop(0, nr // 8, pack_region, 0)
    for side in range(2):
        for j in range(SG):
            send[nr * S + side * SG + j] = cells[gsend[0, side, j]]

    pl.semaphore_wait(barrier, nr + 1)

    def base(table):
        return table.shape[0] - nr * S - 2 * SG

    def region_copy(src, dst, sem, peer):
        return pltpu.make_async_remote_copy(
            src_ref=src.at[pl.ds(peer * S, S)],
            dst_ref=dst.at[pl.ds(base(dst) + r * S, S)],
            send_sem=sems.at[sem],
            recv_sem=sems.at[sem + 1],
            device_id=(g, peer),
            device_id_type=MESH,
        )

    def group_copy(src, dst, sem, side):
        return pltpu.make_async_remote_copy(
            src_ref=src.at[pl.ds(nr * S + side * SG, SG)],
            dst_ref=dst.at[pl.ds(base(dst) + nr * S + (1 - side) * SG, SG)],
            send_sem=sems.at[sem + 2 + 2 * side],
            recv_sem=sems.at[sem + 3 + 2 * side],
            device_id=(up if side else down, r),
            device_id_type=MESH,
        )

    def start_all(src, dst, sem):
        def go(k, carry):
            region_copy(src, dst, sem, far_to_near(k)).start()
            return carry

        lax.fori_loop(0, nr - 1, go, 0)
        group_copy(src, dst, sem, 0).start()
        group_copy(src, dst, sem, 1).start()

    def all_copies(src, dst, sem):
        whole = pltpu.make_async_remote_copy(
            src_ref=src.at[pl.ds(0, (nr - 1) * S)],
            dst_ref=dst.at[pl.ds(base(dst), (nr - 1) * S)],
            send_sem=sems.at[sem],
            recv_sem=sems.at[sem + 1],
            device_id=(g, lax.rem(r + 1, nr)),
            device_id_type=MESH,
        )
        return whole, group_copy(src, dst, sem, 0), group_copy(src, dst, sem, 1)

    def wait_all(src, dst, sem):
        for one in all_copies(src, dst, sem):
            one.wait_recv()

    start_all(send, tbl, 0)
    for load in loads[5:]:
        load.wait()

    count = jnp.full((1, P_SIZE), cnt[0], jnp.int32)
    ids = lax.broadcasted_iota(jnp.int32, (CD, P_SIZE), 0)

    def pack_ratios(out):
        def pack_one(j, carry):
            for u in range(8):
                for s in range(S):
                    at = rsend[0, s, j * 8 + u]
                    out[(j * 8 + u) * S + s] = cown[pl.ds(at, 1), :]
            return carry

        lax.fori_loop(0, nr // 8, pack_one, 0)
        for side in range(2):
            for j in range(SG):
                out[nr * S + side * SG + j] = cown[pl.ds(gsend[0, side, j], 1), :]

    stay = energy[...] / dens[...]
    for i in range(NA):
        stay = jnp.where((ids == act[0, i]) & (count > i), 0.0, stay)
    cown[...] = stay
    pack_ratios(csend0)
    start_all(csend0, ctbl0, 6)

    tbl[pl.ds(CD + r * S, S)] = send[pl.ds(r * S, S)]

    def fill(j, carry):
        at = pl.ds(j * 8, 8)
        tbl[at] = cells[at]
        return carry

    lax.fori_loop(0, CD // 8, fill, 0)
    origin = jnp.concatenate(
        [
            jnp.broadcast_to(jnp.sum(cells[0, 0:3, :], axis=1, keepdims=True) / P_SIZE, (3, P_SIZE)),
            jnp.zeros((1, P_SIZE), jnp.float32),
        ],
        axis=0,
    )

    remap = nb_out[0]
    spread = jnp.full((NA, K), cnt[0], jnp.int32)
    for i in range(NA):
        remap = jnp.where((remap == act[0, i]) & (spread > i), TB + i, remap)
    remapped[0] = remap
    to_scalar = pltpu.make_async_copy(remapped, listed, in_sems.at[len(loads)])
    to_scalar.start()

    point = lax.broadcasted_iota(jnp.int32, (4, P_SIZE), 0) < 3

    def partner_factors(cell):
        a, b, c = three_parts(jnp.concatenate([cell, jnp.where(point, cell * cell, 1.0)], axis=0))
        return jnp.concatenate([a, b, c, a, b, a], axis=0).astype(jnp.bfloat16)

    def partner_weights(cell, ratio):
        base = jnp.where(point, cell * cell[3:4], cell)
        a, b, c = three_parts(jnp.concatenate([base, base * ratio], axis=0))
        return jnp.concatenate([a, b, c, jnp.zeros_like(a)], axis=0).astype(jnp.bfloat16)

    def own_factors(j, carry):
        for u in range(4):
            c = j * 4 + u
            cell = cells[c] - origin
            rhs[c] = partner_factors(cell)
            weights[c] = partner_weights(cell, cown[pl.ds(c, 1), :])
        return carry

    lax.fori_loop(0, CD // 4, own_factors, 0)

    def own_rows(i, carry):
        at = act[0, i]
        cell = cells[at] - origin
        ones = jnp.ones((3, P_SIZE), jnp.float32)
        length = square_length(cell)
        a, b, c = three_parts(
            jnp.concatenate([jnp.where(point, -2.0 * cell, 0.0), ones, length], axis=0)
        )
        wide = jnp.concatenate(
            [a, a, a, b, b, c, jnp.zeros((P_SIZE - 48, P_SIZE), jnp.float32)], axis=0
        )
        lhs[i] = jnp.transpose(wide)[:, 0:48].astype(jnp.bfloat16)
        h = lanes_to_rows(smooth[pl.ds(at, 1), :])
        hbuf[0, i] = h
        hbuf[1, i] = 0.5 * (h * h * h)
        hbuf[2, i] = 0.5 * h
        width = smooth[pl.ds(at, 1), :]
        cube = width * width * width
        rows[0, pl.ds(i, 1), :] = 1.0 / (cube * cube)
        rows[1, pl.ds(i, 1), :] = energy[pl.ds(at, 1), :]
        for f in range(3):
            rows[2 + f, pl.ds(i, 1), :] = cell[f : f + 1]
        mine[i, 0:3, :] = cells[at][0:3]
        mine[i, 3:4, :] = smooth[pl.ds(at, 1), :]
        return carry

    lax.fori_loop(0, NA, own_rows, 0)

    def density_of(i, k, square, m):
        h = hbuf[0, i]
        square = jnp.maximum(square, tiny)
        inv = lax.rsqrt(square)
        d = square * inv
        t = jnp.maximum(h - d, 0.0)
        t2 = t * t
        tbuf[i * NL + k] = t
        qbuf[i * NL + k] = t2
        ibuf[i * NL + k] = inv
        return m * jnp.minimum(t2 * t, hbuf[1, i] - 3.0 * (square * t))

    def density_self(i, carry):
        at = act[0, i]
        square = jnp.dot(lhs[i], rhs[at], preferred_element_type=jnp.float32)
        part[i] = density_of(i, 0, square, cells[at][3:4])
        return carry

    lax.fori_loop(0, NA, density_self, 0)
    wait_all(send, tbl, 0)

    def other_factors(j, carry):
        for u in range(4):
            c = CD + j * 4 + u
            rhs[c] = partner_factors(tbl[c] - origin)
        return carry

    lax.fori_loop(0, (TB - CD) // 4, other_factors, 0)

    def finish_density(i):
        sums[0, pl.ds(i, 1), :] = jnp.sum(jnp.transpose(part[i]), axis=0, keepdims=True)

    def density(i, carry):
        finish_density(lax.rem(i + NA - 1, NA))
        total = part[i]
        for k in range(1, NL, 2):
            first, second = nb[0, i, k - 1], nb[0, i, k]
            square = jnp.dot(
                lhs[i],
                jnp.concatenate([rhs[first], rhs[second]], axis=1),
                preferred_element_type=jnp.float32,
            )
            total += density_of(i, k, square[:, :P_SIZE], tbl[first][3:4])
            total += density_of(i, k + 1, square[:, P_SIZE:], tbl[second][3:4])
        part[i] = total
        return carry

    lax.fori_loop(0, NA, density, 0)
    finish_density(NA - 1)

    slots = lax.broadcasted_iota(jnp.int32, (NA, P_SIZE), 0)
    in_use = slots < count
    rho = density_factor * rows[0] * sums[0]
    rho_out[...] = jnp.where(in_use, rho, 0.0)
    ratio = rows[1] / rho
    rows[5] = ratio
    fresh = stay
    for i in range(NA):
        fresh = jnp.where((ids == act[0, i]) & (count > i), ratio[i : i + 1], fresh)
    cown[...] = fresh
    pack_ratios(csend)

    wait_all(csend0, ctbl0, 6)
    ctbl0[pl.ds(r * S, S)] = csend[pl.ds(r * S, S)]

    known = jnp.concatenate(
        [ctbl0[...].reshape(TB - CD, P_SIZE), jnp.ones((2 * CD - TB, P_SIZE), jnp.float32)], axis=0
    )
    missing = (jnp.transpose(known)[0:1, :] == 0.0).astype(jnp.int32)
    flags[...] = jnp.concatenate([jnp.zeros((1, P_SIZE), jnp.int32), missing], axis=1)
    to_flags = pltpu.make_async_copy(flags, flag, in_sems.at[len(loads) + 1])
    to_flags.start()

    def other_weights(c):
        weights[CD + c] = partner_weights(tbl[CD + c] - origin, ctbl0[c])

    def send_and_weigh(k, carry):
        region_copy(csend, ctbl, 12, far_to_near(k)).start()
        for u in range(5):
            other_weights(k * 5 + u)
        return carry

    lax.fori_loop(0, nr // 2 - 1, send_and_weigh, 0)
    group_copy(csend, ctbl, 12, 0).start()
    group_copy(csend, ctbl, 12, 1).start()
    for c in range(5 * (nr // 2 - 1), TB - CD):
        other_weights(c)
    for i in range(NA):
        at = act[0, i]
        weights[TB + i] = partner_weights(cells[at] - origin, rows[5, i : i + 1, :])
    ctbl[pl.ds(CD + r * S, S)] = csend[pl.ds(r * S, S)]
    to_scalar.wait()
    to_flags.wait()
    def finish_force(i):
        both = jnp.transpose(part[i])
        both = both[0:8] + both[8:16] + both[16:24]
        for f in range(8):
            sums[f, pl.ds(i, 1), :] = both[f : f + 1]

    def force(i, carry):
        finish_force(lax.rem(i + NA - 1, NA))
        h, half = hbuf[0, i], hbuf[2, i]
        total = jnp.zeros((P_SIZE, 32), jnp.float32)
        for k in range(0, NL, 3):
            slopes, wide = [], []
            for at in range(k, k + 3):
                t = tbuf[i * NL + at]
                value = jnp.where(t > half, 3.0 * t - h, qbuf[i * NL + at] * ibuf[i * NL + at])
                a = value.astype(jnp.bfloat16)
                slopes += [a, (value - a.astype(jnp.float32)).astype(jnp.bfloat16)]
                wide += [weights[listed[0, i, at - 1] if at else TB + i]] * 2
            total += lax.dot_general(
                jnp.concatenate(slopes, axis=1),
                jnp.concatenate(wide, axis=1),
                (((1,), (1,)), ((), ())),
                preferred_element_type=jnp.float32,
            )
        part[i, :, 0:32] = total
        hits = 0
        for k in range(K):
            hits += flag[0, listed[0, i, k]] * (1 << k)
        masks[0, i] = hits * jnp.minimum(jnp.maximum(cnt[0] - i, 0), 1)
        return carry

    def send_and_force(i, carry):
        for u in range(4):
            region_copy(csend, ctbl, 12, far_to_near(nr // 2 - 1 + 4 * i + u)).start()
        return force(i, carry)

    lax.fori_loop(0, nr // 8, send_and_force, 0)
    lax.fori_loop(nr // 8, NA, force, 0)
    finish_force(NA - 1)
    to_masks = pltpu.make_async_copy(masks, mask_out, in_sems.at[len(loads) + 2])
    to_masks.start()

    for f in range(3):
        x = rows[2 + f]
        near = x * sums[3] - sums[f]
        far = x * sums[7] - sums[f + 4]
        total = jnp.where(in_use, force_factor * rows[0] * (rows[5] * near + far), 0.0)
        for i in range(NA):
            acc_out[f : f + 1, i * P_SIZE : (i + 1) * P_SIZE] = total[i : i + 1]

    to_masks.wait()
    wait_all(csend, ctbl, 12)
    for src, dst, sem in ((send, tbl, 0), (csend0, ctbl0, 6), (csend, ctbl, 12)):
        for one in all_copies(src, dst, sem):
            one.wait_send()


def late_terms(masks, nb, rho_in, acc_in, tbl, ctbl, mine, rho_out, acc_out):
    rho_out[...] = rho_in[...]
    acc_out[...] = acc_in[...]

    def add(i, c):
        own, other = mine[i], tbl[c]
        h = own[3:4]
        strength = lanes_to_rows(other[3:4] * ctbl[c])
        diff = [own[f : f + 1] - lanes_to_rows(other[f : f + 1]) for f in range(3)]
        square = jnp.maximum(diff[0] * diff[0] + diff[1] * diff[1] + diff[2] * diff[2], tiny)
        inv = lax.rsqrt(square)
        d = square * inv
        t = jnp.maximum(h - d, 0.0)
        weight = strength * jnp.where(t > d, t + t - d, t * t * inv)
        h3 = h * h * h
        scale = force_factor / (h3 * h3)
        at = pl.ds(pl.multiple_of(i * P_SIZE, P_SIZE), P_SIZE)
        for f in range(3):
            acc_out[f : f + 1, at] += scale * jnp.sum(weight * diff[f], axis=0, keepdims=True)

    def slot(i, carry):
        def highest(left):
            k = 31 - lax.clz(left)
            add(i, nb[0, i, k])
            return left - lax.shift_left(1, k)

        lax.while_loop(lambda left: left != 0, highest, masks[0, i])
        return carry

    lax.fori_loop(0, NA, slot, 0)


def body(pos, vel, mass, smooth, energy, dens, act, cnt, nb, rsend, gsend):
    ng, nr = lax.axis_size("group"), lax.axis_size("region")
    square = lambda v: v.reshape(CD, P_SIZE)
    hbm = pl.BlockSpec(memory_space=pltpu.HBM)
    vmem = pl.BlockSpec(memory_space=pltpu.VMEM)
    smem = pl.BlockSpec(memory_space=pltpu.SMEM)
    f32, b16 = jnp.float32, jnp.bfloat16
    args = (
        pos,
        vel,
        square(mass),
        square(smooth),
        square(energy),
        square(dens),
        act,
        cnt,
        nb,
        jnp.transpose(rsend, (0, 2, 1)),
        gsend,
    )
    pin = lambda v: pltpu.with_memory_space_constraint(v, pltpu.HBM)
    args = tuple(v if v is cnt else pin(v) for v in args)
    held = [pltpu.VMEM(v.shape, f32) for v in args[:6]] + [pltpu.SMEM(v.shape, jnp.int32) for v in args[6:]]
    sent = nr * S + 2 * SG
    results = (
        jax.ShapeDtypeStruct((NA, P_SIZE), f32),
        jax.ShapeDtypeStruct((3, NA * P_SIZE), f32),
    )
    rho, acc, table, ratios, masks, mine, near = pl.pallas_call(
        functools.partial(kernel, ng, nr),
        out_shape=results
        + (
            jax.ShapeDtypeStruct((TB, 4, P_SIZE), f32),
            jax.ShapeDtypeStruct((TB, 1, P_SIZE), f32),
            jax.ShapeDtypeStruct((1, NA), jnp.int32),
            jax.ShapeDtypeStruct((NA, 4, P_SIZE), f32),
            jax.ShapeDtypeStruct((1, NA, K), jnp.int32),
        ),
        in_specs=[hbm] * len(args),
        out_specs=(vmem,) * 7,
        scratch_shapes=held
        + [
            pltpu.SMEM((1, NA, K), jnp.int32),
            pltpu.VMEM((1, NA, K), jnp.int32),
            pltpu.VMEM((1, 2 * P_SIZE), jnp.int32),
            pltpu.SMEM((1, 2 * P_SIZE), jnp.int32),
            pltpu.SMEM((1, NA), jnp.int32),
            pltpu.VMEM((CD, 4, P_SIZE), f32),
            pltpu.VMEM((sent, 4, P_SIZE), f32),
            pltpu.VMEM((sent, 1, P_SIZE), f32),
            pltpu.VMEM((sent, 1, P_SIZE), f32),
            pltpu.VMEM((sent, 1, P_SIZE), f32),
            pltpu.VMEM((CD, P_SIZE), f32),
            pltpu.VMEM((TB, 48, P_SIZE), b16),
            pltpu.VMEM((NA, P_SIZE, 48), b16),
            pltpu.VMEM((TB + NA, 32, P_SIZE), b16),
            pltpu.VMEM((3, NA, P_SIZE, P_SIZE), f32),
            pltpu.VMEM((NA, P_SIZE, P_SIZE), f32),
            pltpu.VMEM((6, NA, P_SIZE), f32),
            pltpu.VMEM((8, NA, P_SIZE), f32),
            pltpu.VMEM((NA * NL, P_SIZE, P_SIZE), f32),
            pltpu.VMEM((NA * NL, P_SIZE, P_SIZE), f32),
            pltpu.VMEM((NA * NL, P_SIZE, P_SIZE), f32),
            pltpu.SemaphoreType.DMA((len(args) + 4,)),
            pltpu.SemaphoreType.DMA((18,)),
        ],
        compiler_params=pltpu.CompilerParams(
            collective_id=0, has_side_effects=True, vmem_limit_bytes=50 * 1024 * 1024
        ),
    )(*args)
    rho, acc = pl.pallas_call(
        late_terms,
        out_shape=results,
        in_specs=[smem] * 2 + [vmem] * 5,
        out_specs=(vmem, vmem),
        compiler_params=pltpu.CompilerParams(vmem_limit_bytes=16 * 1024 * 1024),
    )(masks, near, rho, acc, table, ratios, mine)
    return rho.reshape(-1), acc


def solution(mesh):
    both = ("group", "region")
    placed = (
        P(None, both),
        P(None, both),
        P(both),
        P(both),
        P(both),
        P(both),
        P(both, None),
        P(both),
        P(both, None, None),
        P(both, None, None),
        P(both, None, None),
    )
    return jax.shard_map(
        body,
        mesh=mesh,
        in_specs=placed,
        out_specs=(P(both), P(None, both)),
        check_vma=False,
    )
```

```python
import functools
import math

import jax
import jax.numpy as jnp
from jax import lax
from jax.experimental import pallas as pl
from jax.experimental.pallas import tpu as pltpu
from jax.sharding import PartitionSpec as P

P_SIZE = 128
K = 26
S = 2
SG = 8
CD = 128
NA = 8
TB = 208
NL = K + 1
MESH = pl.DeviceIdType.MESH

step_time = 0.1
density_factor = 16.0 / math.pi
force_factor = 32.0 / math.pi
tiny = 1e-30


def lanes_to_rows(row):
    return jnp.transpose(jnp.broadcast_to(row, (P_SIZE, P_SIZE)))


def three_parts(value):
    first = value.astype(jnp.bfloat16).astype(jnp.float32)
    rest = value - first
    second = rest.astype(jnp.bfloat16).astype(jnp.float32)
    return first, second, rest - second


def square_length(cell):
    sq = cell * cell
    return sq[0:1] + sq[1:2] + sq[2:3]


def kernel(
    ng,
    nr,
    pos_in,
    vel_in,
    mass_in,
    smooth_in,
    energy_in,
    dens_in,
    act_in,
    cnt_in,
    nb_in,
    rsend_in,
    gsend_in,
    rho_out,
    acc_out,
    tbl,
    ctbl,
    mask_out,
    mine,
    nb_out,
    pos,
    vel,
    mass,
    smooth,
    energy,
    dens,
    act,
    cnt,
    nb,
    rsend,
    gsend,
    listed,
    remapped,
    flags,
    flag,
    masks,
    cells,
    send,
    ctbl0,
    csend0,
    csend,
    cown,
    rhs,
    lhs,
    weights,
    hbuf,
    part,
    rows,
    sums,
    tbuf,
    qbuf,
    ibuf,
    in_sems,
    sems,
):
    g = lax.axis_index("group")
    r = lax.axis_index("region")
    up = lax.rem(g + 1, ng)
    down = lax.rem(g + ng - 1, ng)
    ny, nz = nr // 8, 8

    loads = [
        pltpu.make_async_copy(src, dst, in_sems.at[n])
        for n, (src, dst) in enumerate(
            (
                (pos_in, pos),
                (vel_in, vel),
                (mass_in, mass),
                (rsend_in, rsend),
                (gsend_in, gsend),
                (energy_in, energy),
                (dens_in, dens),
                (act_in, act),
                (cnt_in, cnt),
                (smooth_in, smooth),
                (nb_in, nb),
                (nb_in, nb_out),
            )
        )
    ]
    def far_to_near(k):
        a, b = lax.div(k, ny), lax.rem(k, ny)
        dz = nz // 2 + lax.div(a + 1, 2) * (1 - 2 * lax.rem(a, 2))
        dy = ny // 2 + lax.div(b + 1, 2) * (1 - 2 * lax.rem(b, 2))
        y, z = lax.div(r, nz), lax.rem(r, nz)
        return lax.rem(y + dy, ny) * nz + lax.rem(z + dz, nz)

    for load in loads:
        load.start()

    barrier = pltpu.get_barrier_semaphore()

    def greet(k, carry):
        pl.semaphore_signal(barrier, inc=1, device_id=(g, far_to_near(k)), device_id_type=MESH)
        return carry

    for k in range(nr - 1):
        greet(k, 0)
    pl.semaphore_signal(barrier, inc=1, device_id=(up, r), device_id_type=MESH)
    pl.semaphore_signal(barrier, inc=1, device_id=(down, r), device_id_type=MESH)

    def drifted(c):
        at = pl.ds(pl.multiple_of(c * P_SIZE, P_SIZE), P_SIZE)
        return pos[:, at] + step_time * vel[:, at]

    def gather(j, carry):
        for u in range(8):
            c = j * 8 + u
            cells[c, 0:3, :] = drifted(c)
            cells[c, 3:4, :] = mass[pl.ds(c, 1), :]
        return carry

    for load in loads[:5]:
        load.wait()
    lax.fori_loop(0, CD // 8, gather, 0)

    def pack_region(j, carry):
        for u in range(8):
            for s in range(S):
                send[(j * 8 + u) * S + s] = cells[rsend[0, s, j * 8 + u]]
        return carry

    lax.fori_loop(0, nr // 8, pack_region, 0)
    for side in range(2):
        for j in range(SG):
            send[nr * S + side * SG + j] = cells[gsend[0, side, j]]

    pl.semaphore_wait(barrier, nr + 1)

    def base(table):
        return table.shape[0] - nr * S - 2 * SG

    def region_copy(src, dst, sem, peer):
        return pltpu.make_async_remote_copy(
            src_ref=src.at[pl.ds(peer * S, S)],
            dst_ref=dst.at[pl.ds(base(dst) + r * S, S)],
            send_sem=sems.at[sem],
            recv_sem=sems.at[sem + 1],
            device_id=(g, peer),
            device_id_type=MESH,
        )

    def group_copy(src, dst, sem, side):
        return pltpu.make_async_remote_copy(
            src_ref=src.at[pl.ds(nr * S + side * SG, SG)],
            dst_ref=dst.at[pl.ds(base(dst) + nr * S + (1 - side) * SG, SG)],
            send_sem=sems.at[sem + 2 + 2 * side],
            recv_sem=sems.at[sem + 3 + 2 * side],
            device_id=(up if side else down, r),
            device_id_type=MESH,
        )

    def start_all(src, dst, sem):
        def go(k, carry):
            region_copy(src, dst, sem, far_to_near(k)).start()
            return carry

        for k in range(nr - 1):
            go(k, 0)
        group_copy(src, dst, sem, 0).start()
        group_copy(src, dst, sem, 1).start()

    def all_copies(src, dst, sem):
        whole = pltpu.make_async_remote_copy(
            src_ref=src.at[pl.ds(0, (nr - 1) * S)],
            dst_ref=dst.at[pl.ds(base(dst), (nr - 1) * S)],
            send_sem=sems.at[sem],
            recv_sem=sems.at[sem + 1],
            device_id=(g, lax.rem(r + 1, nr)),
            device_id_type=MESH,
        )
        return whole, group_copy(src, dst, sem, 0), group_copy(src, dst, sem, 1)

    def wait_all(src, dst, sem):
        for one in all_copies(src, dst, sem):
            one.wait_recv()

    start_all(send, tbl, 0)
    for load in loads[5:]:
        load.wait()

    count = jnp.full((1, P_SIZE), cnt[0], jnp.int32)
    ids = lax.broadcasted_iota(jnp.int32, (CD, P_SIZE), 0)

    def pack_ratios(out):
        def pack_one(j, carry):
            for u in range(8):
                for s in range(S):
                    at = rsend[0, s, j * 8 + u]
                    out[(j * 8 + u) * S + s] = cown[pl.ds(at, 1), :]
            return carry

        lax.fori_loop(0, nr // 8, pack_one, 0)
        for side in range(2):
            for j in range(SG):
                out[nr * S + side * SG + j] = cown[pl.ds(gsend[0, side, j], 1), :]

    stay = energy[...] / dens[...]
    for i in range(NA):
        stay = jnp.where((ids == act[0, i]) & (count > i), 0.0, stay)
    cown[...] = stay
    pack_ratios(csend0)
    start_all(csend0, ctbl0, 6)

    tbl[pl.ds(CD + r * S, S)] = send[pl.ds(r * S, S)]

    def fill(j, carry):
        at = pl.ds(j * 8, 8)
        tbl[at] = cells[at]
        return carry

    lax.fori_loop(0, CD // 8, fill, 0)
    origin = jnp.concatenate(
        [
            jnp.broadcast_to(jnp.sum(cells[0, 0:3, :], axis=1, keepdims=True) / P_SIZE, (3, P_SIZE)),
            jnp.zeros((1, P_SIZE), jnp.float32),
        ],
        axis=0,
    )

    remap = nb_out[0]
    spread = jnp.full((NA, K), cnt[0], jnp.int32)
    for i in range(NA):
        remap = jnp.where((remap == act[0, i]) & (spread > i), TB + i, remap)
    remapped[0] = remap
    to_scalar = pltpu.make_async_copy(remapped, listed, in_sems.at[len(loads)])
    to_scalar.start()

    point = lax.broadcasted_iota(jnp.int32, (4, P_SIZE), 0) < 3

    def partner_factors(cell):
        a, b, c = three_parts(jnp.concatenate([cell, jnp.where(point, cell * cell, 1.0)], axis=0))
        return jnp.concatenate([a, b, c, a, b, a], axis=0).astype(jnp.bfloat16)

    def partner_weights(cell, ratio):
        base = jnp.where(point, cell * cell[3:4], cell)
        a, b, c = three_parts(jnp.concatenate([base, base * ratio], axis=0))
        return jnp.concatenate([a, b, c, jnp.zeros_like(a)], axis=0).astype(jnp.bfloat16)

    def own_factors(j, carry):
        for u in range(4):
            c = j * 4 + u
            cell = cells[c] - origin
            rhs[c] = partner_factors(cell)
            weights[c] = partner_weights(cell, cown[pl.ds(c, 1), :])
        return carry

    lax.fori_loop(0, CD // 4, own_factors, 0)

    def own_rows(i, carry):
        at = act[0, i]
        cell = cells[at] - origin
        ones = jnp.ones((3, P_SIZE), jnp.float32)
        length = square_length(cell)
        a, b, c = three_parts(
            jnp.concatenate([jnp.where(point, -2.0 * cell, 0.0), ones, length], axis=0)
        )
        wide = jnp.concatenate(
            [a, a, a, b, b, c, jnp.zeros((P_SIZE - 48, P_SIZE), jnp.float32)], axis=0
        )
        lhs[i] = jnp.transpose(wide)[:, 0:48].astype(jnp.bfloat16)
        h = lanes_to_rows(smooth[pl.ds(at, 1), :])
        hbuf[0, i] = h
        hbuf[1, i] = 0.5 * (h * h * h)
        hbuf[2, i] = 0.5 * h
        width = smooth[pl.ds(at, 1), :]
        cube = width * width * width
        rows[0, pl.ds(i, 1), :] = 1.0 / (cube * cube)
        rows[1, pl.ds(i, 1), :] = energy[pl.ds(at, 1), :]
        for f in range(3):
            rows[2 + f, pl.ds(i, 1), :] = cell[f : f + 1]
        mine[i, 0:3, :] = cells[at][0:3]
        mine[i, 3:4, :] = smooth[pl.ds(at, 1), :]
        return carry

    lax.fori_loop(0, NA, own_rows, 0)

    def density_of(i, k, square, m):
        h = hbuf[0, i]
        square = jnp.maximum(square, tiny)
        inv = lax.rsqrt(square)
        d = square * inv
        t = jnp.maximum(h - d, 0.0)
        t2 = t * t
        tbuf[i * NL + k] = t
        qbuf[i * NL + k] = t2
        ibuf[i * NL + k] = inv
        return m * jnp.minimum(t2 * t, hbuf[1, i] - 3.0 * (square * t))

    def density_self(i, carry):
        at = act[0, i]
        square = jnp.dot(lhs[i], rhs[at], preferred_element_type=jnp.float32)
        part[i] = density_of(i, 0, square, cells[at][3:4])
        return carry

    lax.fori_loop(0, NA, density_self, 0)
    wait_all(send, tbl, 0)

    def other_factors(j, carry):
        for u in range(4):
            c = CD + j * 4 + u
            rhs[c] = partner_factors(tbl[c] - origin)
        return carry

    lax.fori_loop(0, (TB - CD) // 4, other_factors, 0)

    def finish_density(i):
        sums[0, pl.ds(i, 1), :] = jnp.sum(jnp.transpose(part[i]), axis=0, keepdims=True)

    def density(i, carry):
        finish_density(lax.rem(i + NA - 1, NA))
        total = part[i]
        for k in range(1, NL, 2):
            first, second = nb[0, i, k - 1], nb[0, i, k]
            square = jnp.dot(
                lhs[i],
                jnp.concatenate([rhs[first], rhs[second]], axis=1),
                preferred_element_type=jnp.float32,
            )
            total += density_of(i, k, square[:, :P_SIZE], tbl[first][3:4])
            total += density_of(i, k + 1, square[:, P_SIZE:], tbl[second][3:4])
        part[i] = total
        return carry

    lax.fori_loop(0, NA, density, 0)
    finish_density(NA - 1)

    slots = lax.broadcasted_iota(jnp.int32, (NA, P_SIZE), 0)
    in_use = slots < count
    rho = density_factor * rows[0] * sums[0]
    rho_out[...] = jnp.where(in_use, rho, 0.0)
    ratio = rows[1] / rho
    rows[5] = ratio
    fresh = stay
    for i in range(NA):
        fresh = jnp.where((ids == act[0, i]) & (count > i), ratio[i : i + 1], fresh)
    cown[...] = fresh
    pack_ratios(csend)

    wait_all(csend0, ctbl0, 6)
    ctbl0[pl.ds(r * S, S)] = csend[pl.ds(r * S, S)]

    known = jnp.concatenate(
        [ctbl0[...].reshape(TB - CD, P_SIZE), jnp.ones((2 * CD - TB, P_SIZE), jnp.float32)], axis=0
    )
    missing = (jnp.transpose(known)[0:1, :] == 0.0).astype(jnp.int32)
    flags[...] = jnp.concatenate([jnp.zeros((1, P_SIZE), jnp.int32), missing], axis=1)
    to_flags = pltpu.make_async_copy(flags, flag, in_sems.at[len(loads) + 1])
    to_flags.start()

    def other_weights(c):
        weights[CD + c] = partner_weights(tbl[CD + c] - origin, ctbl0[c])

    def send_and_weigh(k, carry):
        region_copy(csend, ctbl, 12, far_to_near(k)).start()
        for u in range(5):
            other_weights(k * 5 + u)
        return carry

    for k in range(nr // 2 - 1):
        send_and_weigh(k, 0)
    group_copy(csend, ctbl, 12, 0).start()
    group_copy(csend, ctbl, 12, 1).start()
    for c in range(5 * (nr // 2 - 1), TB - CD):
        other_weights(c)
    for i in range(NA):
        at = act[0, i]
        weights[TB + i] = partner_weights(cells[at] - origin, rows[5, i : i + 1, :])
    ctbl[pl.ds(CD + r * S, S)] = csend[pl.ds(r * S, S)]
    to_scalar.wait()
    to_flags.wait()
    def finish_force(i):
        both = jnp.transpose(part[i])
        both = both[0:8] + both[8:16] + both[16:24]
        for f in range(8):
            sums[f, pl.ds(i, 1), :] = both[f : f + 1]

    def force(i, carry):
        finish_force(lax.rem(i + NA - 1, NA))
        h, half = hbuf[0, i], hbuf[2, i]
        total = jnp.zeros((P_SIZE, 32), jnp.float32)
        for k in range(0, NL, 3):
            slopes, wide = [], []
            for at in range(k, k + 3):
                t = tbuf[i * NL + at]
                value = jnp.where(t > half, 3.0 * t - h, qbuf[i * NL + at] * ibuf[i * NL + at])
                a = value.astype(jnp.bfloat16)
                slopes += [a, (value - a.astype(jnp.float32)).astype(jnp.bfloat16)]
                wide += [weights[listed[0, i, at - 1] if at else TB + i]] * 2
            total += lax.dot_general(
                jnp.concatenate(slopes, axis=1),
                jnp.concatenate(wide, axis=1),
                (((1,), (1,)), ((), ())),
                preferred_element_type=jnp.float32,
            )
        part[i, :, 0:32] = total
        hits = 0
        for k in range(K):
            hits += flag[0, listed[0, i, k]] * (1 << k)
        masks[0, i] = hits * jnp.minimum(jnp.maximum(cnt[0] - i, 0), 1)
        return carry

    def send_and_force(i, carry):
        for u in range(4):
            region_copy(csend, ctbl, 12, far_to_near(nr // 2 - 1 + 4 * i + u)).start()
        return force(i, carry)

    lax.fori_loop(0, nr // 8, send_and_force, 0)
    lax.fori_loop(nr // 8, NA, force, 0)
    finish_force(NA - 1)
    to_masks = pltpu.make_async_copy(masks, mask_out, in_sems.at[len(loads) + 2])
    to_masks.start()

    for f in range(3):
        x = rows[2 + f]
        near = x * sums[3] - sums[f]
        far = x * sums[7] - sums[f + 4]
        total = jnp.where(in_use, force_factor * rows[0] * (rows[5] * near + far), 0.0)
        for i in range(NA):
            acc_out[f : f + 1, i * P_SIZE : (i + 1) * P_SIZE] = total[i : i + 1]

    to_masks.wait()
    wait_all(csend, ctbl, 12)
    for src, dst, sem in ((send, tbl, 0), (csend0, ctbl0, 6), (csend, ctbl, 12)):
        for one in all_copies(src, dst, sem):
            one.wait_send()


def late_terms(masks, nb, rho_in, acc_in, tbl, ctbl, mine, rho_out, acc_out):
    rho_out[...] = rho_in[...]
    acc_out[...] = acc_in[...]

    def add(i, c):
        own, other = mine[i], tbl[c]
        h = own[3:4]
        strength = lanes_to_rows(other[3:4] * ctbl[c])
        diff = [own[f : f + 1] - lanes_to_rows(other[f : f + 1]) for f in range(3)]
        square = jnp.maximum(diff[0] * diff[0] + diff[1] * diff[1] + diff[2] * diff[2], tiny)
        inv = lax.rsqrt(square)
        d = square * inv
        t = jnp.maximum(h - d, 0.0)
        weight = strength * jnp.where(t > d, t + t - d, t * t * inv)
        h3 = h * h * h
        scale = force_factor / (h3 * h3)
        at = pl.ds(pl.multiple_of(i * P_SIZE, P_SIZE), P_SIZE)
        for f in range(3):
            acc_out[f : f + 1, at] += scale * jnp.sum(weight * diff[f], axis=0, keepdims=True)

    def slot(i, carry):
        def highest(left):
            k = 31 - lax.clz(left)
            add(i, nb[0, i, k])
            return left - lax.shift_left(1, k)

        lax.while_loop(lambda left: left != 0, highest, masks[0, i])
        return carry

    lax.fori_loop(0, NA, slot, 0)


def body(pos, vel, mass, smooth, energy, dens, act, cnt, nb, rsend, gsend):
    ng, nr = lax.axis_size("group"), lax.axis_size("region")
    square = lambda v: v.reshape(CD, P_SIZE)
    hbm = pl.BlockSpec(memory_space=pltpu.HBM)
    vmem = pl.BlockSpec(memory_space=pltpu.VMEM)
    smem = pl.BlockSpec(memory_space=pltpu.SMEM)
    f32, b16 = jnp.float32, jnp.bfloat16
    args = (
        pos,
        vel,
        square(mass),
        square(smooth),
        square(energy),
        square(dens),
        act,
        cnt,
        nb,
        jnp.transpose(rsend, (0, 2, 1)),
        gsend,
    )
    pin = lambda v: pltpu.with_memory_space_constraint(v, pltpu.HBM)
    args = tuple(v if v is cnt else pin(v) for v in args)
    held = [pltpu.VMEM(v.shape, f32) for v in args[:6]] + [pltpu.SMEM(v.shape, jnp.int32) for v in args[6:]]
    sent = nr * S + 2 * SG
    results = (
        jax.ShapeDtypeStruct((NA, P_SIZE), f32),
        jax.ShapeDtypeStruct((3, NA * P_SIZE), f32),
    )
    rho, acc, table, ratios, masks, mine, near = pl.pallas_call(
        functools.partial(kernel, ng, nr),
        out_shape=results
        + (
            jax.ShapeDtypeStruct((TB, 4, P_SIZE), f32),
            jax.ShapeDtypeStruct((TB, 1, P_SIZE), f32),
            jax.ShapeDtypeStruct((1, NA), jnp.int32),
            jax.ShapeDtypeStruct((NA, 4, P_SIZE), f32),
            jax.ShapeDtypeStruct((1, NA, K), jnp.int32),
        ),
        in_specs=[hbm] * len(args),
        out_specs=(vmem,) * 7,
        scratch_shapes=held
        + [
            pltpu.SMEM((1, NA, K), jnp.int32),
            pltpu.VMEM((1, NA, K), jnp.int32),
            pltpu.VMEM((1, 2 * P_SIZE), jnp.int32),
            pltpu.SMEM((1, 2 * P_SIZE), jnp.int32),
            pltpu.SMEM((1, NA), jnp.int32),
            pltpu.VMEM((CD, 4, P_SIZE), f32),
            pltpu.VMEM((sent, 4, P_SIZE), f32),
            pltpu.VMEM((sent, 1, P_SIZE), f32),
            pltpu.VMEM((sent, 1, P_SIZE), f32),
            pltpu.VMEM((sent, 1, P_SIZE), f32),
            pltpu.VMEM((CD, P_SIZE), f32),
            pltpu.VMEM((TB, 48, P_SIZE), b16),
            pltpu.VMEM((NA, P_SIZE, 48), b16),
            pltpu.VMEM((TB + NA, 32, P_SIZE), b16),
            pltpu.VMEM((3, NA, P_SIZE, P_SIZE), f32),
            pltpu.VMEM((NA, P_SIZE, P_SIZE), f32),
            pltpu.VMEM((6, NA, P_SIZE), f32),
            pltpu.VMEM((8, NA, P_SIZE), f32),
            pltpu.VMEM((NA * NL, P_SIZE, P_SIZE), f32),
            pltpu.VMEM((NA * NL, P_SIZE, P_SIZE), f32),
            pltpu.VMEM((NA * NL, P_SIZE, P_SIZE), f32),
            pltpu.SemaphoreType.DMA((len(args) + 4,)),
            pltpu.SemaphoreType.DMA((18,)),
        ],
        compiler_params=pltpu.CompilerParams(
            collective_id=0, has_side_effects=True, vmem_limit_bytes=50 * 1024 * 1024
        ),
    )(*args)
    rho, acc = pl.pallas_call(
        late_terms,
        out_shape=results,
        in_specs=[smem] * 2 + [vmem] * 5,
        out_specs=(vmem, vmem),
        compiler_params=pltpu.CompilerParams(vmem_limit_bytes=16 * 1024 * 1024),
    )(masks, near, rho, acc, table, ratios, mine)
    return rho.reshape(-1), acc


def solution(mesh):
    both = ("group", "region")
    placed = (
        P(None, both),
        P(None, both),
        P(both),
        P(both),
        P(both),
        P(both),
        P(both, None),
        P(both),
        P(both, None, None),
        P(both, None, None),
        P(both, None, None),
    )
    return jax.shard_map(
        body,
        mesh=mesh,
        in_specs=placed,
        out_specs=(P(both), P(None, both)),
        check_vma=False,
    )
```

```python
import functools
import math

import jax
import jax.numpy as jnp
from jax import lax
from jax.experimental import pallas as pl
from jax.experimental.pallas import tpu as pltpu
from jax.sharding import PartitionSpec as P

P_SIZE = 128
K = 26
S = 2
SG = 8
CD = 128
NA = 8
TB = 208
NL = K + 1
MESH = pl.DeviceIdType.MESH

step_time = 0.1
density_factor = 16.0 / math.pi
force_factor = 32.0 / math.pi
tiny = 1e-30


def lanes_to_rows(row):
    return jnp.transpose(jnp.broadcast_to(row, (P_SIZE, P_SIZE)))


def three_parts(value):
    first = value.astype(jnp.bfloat16).astype(jnp.float32)
    rest = value - first
    second = rest.astype(jnp.bfloat16).astype(jnp.float32)
    return first, second, rest - second


def square_length(cell):
    sq = cell * cell
    return sq[0:1] + sq[1:2] + sq[2:3]


def kernel(
    ng,
    nr,
    pos_in,
    vel_in,
    mass_in,
    smooth_in,
    energy_in,
    dens_in,
    act_in,
    cnt_in,
    nb_in,
    rsend_in,
    gsend_in,
    rho_out,
    acc_out,
    tbl,
    ctbl,
    mask_out,
    mine,
    nb_out,
    pos,
    vel,
    mass,
    smooth,
    energy,
    dens,
    act,
    cnt,
    nb,
    rsend,
    gsend,
    listed,
    remapped,
    flags,
    flag,
    masks,
    cells,
    send,
    ctbl0,
    csend0,
    csend,
    cown,
    rhs,
    lhs,
    weights,
    hbuf,
    part,
    rows,
    sums,
    tbuf,
    qbuf,
    ibuf,
    in_sems,
    sems,
):
    g = lax.axis_index("group")
    r = lax.axis_index("region")
    up = lax.rem(g + 1, ng)
    down = lax.rem(g + ng - 1, ng)
    ny, nz = nr // 8, 8

    loads = [
        pltpu.make_async_copy(src, dst, in_sems.at[n])
        for n, (src, dst) in enumerate(
            (
                (pos_in, pos),
                (vel_in, vel),
                (mass_in, mass),
                (rsend_in, rsend),
                (gsend_in, gsend),
                (energy_in, energy),
                (dens_in, dens),
                (act_in, act),
                (cnt_in, cnt),
                (smooth_in, smooth),
                (nb_in, nb),
                (nb_in, nb_out),
            )
        )
    ]
    def far_to_near(k):
        a, b = lax.div(k, ny), lax.rem(k, ny)
        dz = nz // 2 + lax.div(a + 1, 2) * (1 - 2 * lax.rem(a, 2))
        dy = ny // 2 + lax.div(b + 1, 2) * (1 - 2 * lax.rem(b, 2))
        y, z = lax.div(r, nz), lax.rem(r, nz)
        return lax.rem(y + dy, ny) * nz + lax.rem(z + dz, nz)

    for load in loads:
        load.start()

    barrier = pltpu.get_barrier_semaphore()

    def greet(k, carry):
        pl.semaphore_signal(barrier, inc=1, device_id=(g, far_to_near(k)), device_id_type=MESH)
        return carry

    for k in range(nr - 1):
        greet(k, 0)
    pl.semaphore_signal(barrier, inc=1, device_id=(up, r), device_id_type=MESH)
    pl.semaphore_signal(barrier, inc=1, device_id=(down, r), device_id_type=MESH)

    def drifted(c):
        at = pl.ds(pl.multiple_of(c * P_SIZE, P_SIZE), P_SIZE)
        return pos[:, at] + step_time * vel[:, at]

    def gather(j, carry):
        for u in range(8):
            c = j * 8 + u
            cells[c, 0:3, :] = drifted(c)
            cells[c, 3:4, :] = mass[pl.ds(c, 1), :]
        return carry

    for load in loads[:5]:
        load.wait()
    lax.fori_loop(0, CD // 8, gather, 0)

    def pack_region(j, carry):
        for u in range(8):
            for s in range(S):
                send[(j * 8 + u) * S + s] = cells[rsend[0, s, j * 8 + u]]
        return carry

    lax.fori_loop(0, nr // 8, pack_region, 0)
    for side in range(2):
        for j in range(SG):
            send[nr * S + side * SG + j] = cells[gsend[0, side, j]]

    pl.semaphore_wait(barrier, nr + 1)

    def base(table):
        return table.shape[0] - nr * S - 2 * SG

    def region_copy(src, dst, sem, peer):
        return pltpu.make_async_remote_copy(
            src_ref=src.at[pl.ds(peer * S, S)],
            dst_ref=dst.at[pl.ds(base(dst) + r * S, S)],
            send_sem=sems.at[sem],
            recv_sem=sems.at[sem + 1],
            device_id=(g, peer),
            device_id_type=MESH,
        )

    def group_copy(src, dst, sem, side):
        return pltpu.make_async_remote_copy(
            src_ref=src.at[pl.ds(nr * S + side * SG, SG)],
            dst_ref=dst.at[pl.ds(base(dst) + nr * S + (1 - side) * SG, SG)],
            send_sem=sems.at[sem + 2 + 2 * side],
            recv_sem=sems.at[sem + 3 + 2 * side],
            device_id=(up if side else down, r),
            device_id_type=MESH,
        )

    def start_all(src, dst, sem):
        def go(k, carry):
            region_copy(src, dst, sem, far_to_near(k)).start()
            return carry

        for k in range(nr - 1):
            go(k, 0)
        group_copy(src, dst, sem, 0).start()
        group_copy(src, dst, sem, 1).start()

    def all_copies(src, dst, sem):
        whole = pltpu.make_async_remote_copy(
            src_ref=src.at[pl.ds(0, (nr - 1) * S)],
            dst_ref=dst.at[pl.ds(base(dst), (nr - 1) * S)],
            send_sem=sems.at[sem],
            recv_sem=sems.at[sem + 1],
            device_id=(g, lax.rem(r + 1, nr)),
            device_id_type=MESH,
        )
        return whole, group_copy(src, dst, sem, 0), group_copy(src, dst, sem, 1)

    def wait_all(src, dst, sem):
        for one in all_copies(src, dst, sem):
            one.wait_recv()

    start_all(send, tbl, 0)
    for load in loads[5:]:
        load.wait()

    count = jnp.full((1, P_SIZE), cnt[0], jnp.int32)
    ids = lax.broadcasted_iota(jnp.int32, (CD, P_SIZE), 0)

    def pack_ratios(out):
        def pack_one(j, carry):
            for u in range(8):
                for s in range(S):
                    at = rsend[0, s, j * 8 + u]
                    out[(j * 8 + u) * S + s] = cown[pl.ds(at, 1), :]
            return carry

        lax.fori_loop(0, nr // 8, pack_one, 0)
        for side in range(2):
            for j in range(SG):
                out[nr * S + side * SG + j] = cown[pl.ds(gsend[0, side, j], 1), :]

    stay = energy[...] / dens[...]
    for i in range(NA):
        stay = jnp.where((ids == act[0, i]) & (count > i), 0.0, stay)
    cown[...] = stay
    pack_ratios(csend0)
    start_all(csend0, ctbl0, 6)

    tbl[pl.ds(CD + r * S, S)] = send[pl.ds(r * S, S)]

    def fill(j, carry):
        at = pl.ds(j * 8, 8)
        tbl[at] = cells[at]
        return carry

    lax.fori_loop(0, CD // 8, fill, 0)
    origin = jnp.concatenate(
        [
            jnp.broadcast_to(jnp.sum(cells[0, 0:3, :], axis=1, keepdims=True) / P_SIZE, (3, P_SIZE)),
            jnp.zeros((1, P_SIZE), jnp.float32),
        ],
        axis=0,
    )

    remap = nb_out[0]
    spread = jnp.full((NA, K), cnt[0], jnp.int32)
    for i in range(NA):
        remap = jnp.where((remap == act[0, i]) & (spread > i), TB + i, remap)
    remapped[0] = remap
    to_scalar = pltpu.make_async_copy(remapped, listed, in_sems.at[len(loads)])
    to_scalar.start()

    point = lax.broadcasted_iota(jnp.int32, (4, P_SIZE), 0) < 3

    def partner_factors(cell):
        a, b, c = three_parts(jnp.concatenate([cell, jnp.where(point, cell * cell, 1.0)], axis=0))
        return jnp.concatenate([a, b, c, a, b, a], axis=0).astype(jnp.bfloat16)

    def partner_weights(cell, ratio):
        base = jnp.where(point, cell * cell[3:4], cell)
        a, b, c = three_parts(jnp.concatenate([base, base * ratio], axis=0))
        return jnp.concatenate([a, b, c, jnp.zeros_like(a)], axis=0).astype(jnp.bfloat16)

    def own_factors(j, carry):
        for u in range(4):
            c = j * 4 + u
            cell = cells[c] - origin
            rhs[c] = partner_factors(cell)
            weights[c] = partner_weights(cell, cown[pl.ds(c, 1), :])
        return carry

    lax.fori_loop(0, CD // 4, own_factors, 0)

    def own_rows(i, carry):
        at = act[0, i]
        cell = cells[at] - origin
        ones = jnp.ones((3, P_SIZE), jnp.float32)
        length = square_length(cell)
        a, b, c = three_parts(
            jnp.concatenate([jnp.where(point, -2.0 * cell, 0.0), ones, length], axis=0)
        )
        wide = jnp.concatenate(
            [a, a, a, b, b, c, jnp.zeros((P_SIZE - 48, P_SIZE), jnp.float32)], axis=0
        )
        lhs[i] = jnp.transpose(wide)[:, 0:48].astype(jnp.bfloat16)
        h = lanes_to_rows(smooth[pl.ds(at, 1), :])
        hbuf[0, i] = h
        hbuf[1, i] = 0.5 * (h * h * h)
        hbuf[2, i] = 0.5 * h
        width = smooth[pl.ds(at, 1), :]
        cube = width * width * width
        rows[0, pl.ds(i, 1), :] = 1.0 / (cube * cube)
        rows[1, pl.ds(i, 1), :] = energy[pl.ds(at, 1), :]
        for f in range(3):
            rows[2 + f, pl.ds(i, 1), :] = cell[f : f + 1]
        mine[i, 0:3, :] = cells[at][0:3]
        mine[i, 3:4, :] = smooth[pl.ds(at, 1), :]
        return carry

    lax.fori_loop(0, NA, own_rows, 0)

    def density_of(i, k, square, m):
        h = hbuf[0, i]
        square = jnp.maximum(square, tiny)
        inv = lax.rsqrt(square)
        d = square * inv
        t = jnp.maximum(h - d, 0.0)
        t2 = t * t
        tbuf[i * NL + k] = t
        qbuf[i * NL + k] = t2
        ibuf[i * NL + k] = inv
        return m * jnp.minimum(t2 * t, hbuf[1, i] - 3.0 * (square * t))

    def density_self(i, carry):
        at = act[0, i]
        square = jnp.dot(lhs[i], rhs[at], preferred_element_type=jnp.float32)
        part[i] = density_of(i, 0, square, cells[at][3:4])
        return carry

    lax.fori_loop(0, NA, density_self, 0)
    wait_all(send, tbl, 0)

    def other_factors(j, carry):
        for u in range(4):
            c = CD + j * 4 + u
            rhs[c] = partner_factors(tbl[c] - origin)
        return carry

    lax.fori_loop(0, (TB - CD) // 4, other_factors, 0)

    def finish_density(i):
        sums[0, pl.ds(i, 1), :] = jnp.sum(jnp.transpose(part[i]), axis=0, keepdims=True)

    def density(i, carry):
        finish_density(lax.rem(i + NA - 1, NA))
        total = part[i]
        for k in range(1, NL, 2):
            first, second = nb[0, i, k - 1], nb[0, i, k]
            square = jnp.dot(
                lhs[i],
                jnp.concatenate([rhs[first], rhs[second]], axis=1),
                preferred_element_type=jnp.float32,
            )
            total += density_of(i, k, square[:, :P_SIZE], tbl[first][3:4])
            total += density_of(i, k + 1, square[:, P_SIZE:], tbl[second][3:4])
        part[i] = total
        return carry

    lax.fori_loop(0, NA, density, 0)
    finish_density(NA - 1)

    slots = lax.broadcasted_iota(jnp.int32, (NA, P_SIZE), 0)
    in_use = slots < count
    rho = density_factor * rows[0] * sums[0]
    rho_out[...] = jnp.where(in_use, rho, 0.0)
    ratio = rows[1] / rho
    rows[5] = ratio
    fresh = stay
    for i in range(NA):
        fresh = jnp.where((ids == act[0, i]) & (count > i), ratio[i : i + 1], fresh)
    cown[...] = fresh
    pack_ratios(csend)

    wait_all(csend0, ctbl0, 6)
    ctbl0[pl.ds(r * S, S)] = csend[pl.ds(r * S, S)]

    known = jnp.concatenate(
        [ctbl0[...].reshape(TB - CD, P_SIZE), jnp.ones((2 * CD - TB, P_SIZE), jnp.float32)], axis=0
    )
    missing = (jnp.transpose(known)[0:1, :] == 0.0).astype(jnp.int32)
    flags[...] = jnp.concatenate([jnp.zeros((1, P_SIZE), jnp.int32), missing], axis=1)
    to_flags = pltpu.make_async_copy(flags, flag, in_sems.at[len(loads) + 1])
    to_flags.start()

    def other_weights(c):
        weights[CD + c] = partner_weights(tbl[CD + c] - origin, ctbl0[c])

    def send_and_weigh(k, carry):
        region_copy(csend, ctbl, 12, far_to_near(k)).start()
        return carry

    for k in range(nr - 1):
        send_and_weigh(k, 0)
    group_copy(csend, ctbl, 12, 0).start()
    group_copy(csend, ctbl, 12, 1).start()
    def more_weights(j, carry):
        for u in range(8):
            other_weights(j * 8 + u)
        return carry

    lax.fori_loop(0, (TB - CD) // 8, more_weights, 0)
    for i in range(NA):
        at = act[0, i]
        weights[TB + i] = partner_weights(cells[at] - origin, rows[5, i : i + 1, :])
    ctbl[pl.ds(CD + r * S, S)] = csend[pl.ds(r * S, S)]
    to_scalar.wait()
    to_flags.wait()
    def finish_force(i):
        both = jnp.transpose(part[i])
        both = both[0:8] + both[8:16] + both[16:24]
        for f in range(8):
            sums[f, pl.ds(i, 1), :] = both[f : f + 1]

    def force(i, carry):
        finish_force(lax.rem(i + NA - 1, NA))
        h, half = hbuf[0, i], hbuf[2, i]
        total = jnp.zeros((P_SIZE, 32), jnp.float32)
        for k in range(0, NL, 3):
            slopes, wide = [], []
            for at in range(k, k + 3):
                t = tbuf[i * NL + at]
                value = jnp.where(t > half, 3.0 * t - h, qbuf[i * NL + at] * ibuf[i * NL + at])
                a = value.astype(jnp.bfloat16)
                slopes += [a, (value - a.astype(jnp.float32)).astype(jnp.bfloat16)]
                wide += [weights[listed[0, i, at - 1] if at else TB + i]] * 2
            total += lax.dot_general(
                jnp.concatenate(slopes, axis=1),
                jnp.concatenate(wide, axis=1),
                (((1,), (1,)), ((), ())),
                preferred_element_type=jnp.float32,
            )
        part[i, :, 0:32] = total
        hits = 0
        for k in range(K):
            hits += flag[0, listed[0, i, k]] * (1 << k)
        masks[0, i] = hits * jnp.minimum(jnp.maximum(cnt[0] - i, 0), 1)
        return carry

    lax.fori_loop(0, NA, force, 0)
    finish_force(NA - 1)
    to_masks = pltpu.make_async_copy(masks, mask_out, in_sems.at[len(loads) + 2])
    to_masks.start()

    for f in range(3):
        x = rows[2 + f]
        near = x * sums[3] - sums[f]
        far = x * sums[7] - sums[f + 4]
        total = jnp.where(in_use, force_factor * rows[0] * (rows[5] * near + far), 0.0)
        for i in range(NA):
            acc_out[f : f + 1, i * P_SIZE : (i + 1) * P_SIZE] = total[i : i + 1]

    to_masks.wait()
    wait_all(csend, ctbl, 12)
    for src, dst, sem in ((send, tbl, 0), (csend0, ctbl0, 6), (csend, ctbl, 12)):
        for one in all_copies(src, dst, sem):
            one.wait_send()


def late_terms(masks, nb, rho_in, acc_in, tbl, ctbl, mine, rho_out, acc_out):
    rho_out[...] = rho_in[...]
    acc_out[...] = acc_in[...]

    def add(i, c):
        own, other = mine[i], tbl[c]
        h = own[3:4]
        strength = lanes_to_rows(other[3:4] * ctbl[c])
        diff = [own[f : f + 1] - lanes_to_rows(other[f : f + 1]) for f in range(3)]
        square = jnp.maximum(diff[0] * diff[0] + diff[1] * diff[1] + diff[2] * diff[2], tiny)
        inv = lax.rsqrt(square)
        d = square * inv
        t = jnp.maximum(h - d, 0.0)
        weight = strength * jnp.where(t > d, t + t - d, t * t * inv)
        h3 = h * h * h
        scale = force_factor / (h3 * h3)
        at = pl.ds(pl.multiple_of(i * P_SIZE, P_SIZE), P_SIZE)
        for f in range(3):
            acc_out[f : f + 1, at] += scale * jnp.sum(weight * diff[f], axis=0, keepdims=True)

    def slot(i, carry):
        def highest(left):
            k = 31 - lax.clz(left)
            add(i, nb[0, i, k])
            return left - lax.shift_left(1, k)

        lax.while_loop(lambda left: left != 0, highest, masks[0, i])
        return carry

    lax.fori_loop(0, NA, slot, 0)


def body(pos, vel, mass, smooth, energy, dens, act, cnt, nb, rsend, gsend):
    ng, nr = lax.axis_size("group"), lax.axis_size("region")
    square = lambda v: v.reshape(CD, P_SIZE)
    hbm = pl.BlockSpec(memory_space=pltpu.HBM)
    vmem = pl.BlockSpec(memory_space=pltpu.VMEM)
    smem = pl.BlockSpec(memory_space=pltpu.SMEM)
    f32, b16 = jnp.float32, jnp.bfloat16
    args = (
        pos,
        vel,
        square(mass),
        square(smooth),
        square(energy),
        square(dens),
        act,
        cnt,
        nb,
        jnp.transpose(rsend, (0, 2, 1)),
        gsend,
    )
    pin = lambda v: pltpu.with_memory_space_constraint(v, pltpu.HBM)
    args = tuple(v if v is cnt else pin(v) for v in args)
    held = [pltpu.VMEM(v.shape, f32) for v in args[:6]] + [pltpu.SMEM(v.shape, jnp.int32) for v in args[6:]]
    sent = nr * S + 2 * SG
    results = (
        jax.ShapeDtypeStruct((NA, P_SIZE), f32),
        jax.ShapeDtypeStruct((3, NA * P_SIZE), f32),
    )
    rho, acc, table, ratios, masks, mine, near = pl.pallas_call(
        functools.partial(kernel, ng, nr),
        out_shape=results
        + (
            jax.ShapeDtypeStruct((TB, 4, P_SIZE), f32),
            jax.ShapeDtypeStruct((TB, 1, P_SIZE), f32),
            jax.ShapeDtypeStruct((1, NA), jnp.int32),
            jax.ShapeDtypeStruct((NA, 4, P_SIZE), f32),
            jax.ShapeDtypeStruct((1, NA, K), jnp.int32),
        ),
        in_specs=[hbm] * len(args),
        out_specs=(vmem,) * 7,
        scratch_shapes=held
        + [
            pltpu.SMEM((1, NA, K), jnp.int32),
            pltpu.VMEM((1, NA, K), jnp.int32),
            pltpu.VMEM((1, 2 * P_SIZE), jnp.int32),
            pltpu.SMEM((1, 2 * P_SIZE), jnp.int32),
            pltpu.SMEM((1, NA), jnp.int32),
            pltpu.VMEM((CD, 4, P_SIZE), f32),
            pltpu.VMEM((sent, 4, P_SIZE), f32),
            pltpu.VMEM((sent, 1, P_SIZE), f32),
            pltpu.VMEM((sent, 1, P_SIZE), f32),
            pltpu.VMEM((sent, 1, P_SIZE), f32),
            pltpu.VMEM((CD, P_SIZE), f32),
            pltpu.VMEM((TB, 48, P_SIZE), b16),
            pltpu.VMEM((NA, P_SIZE, 48), b16),
            pltpu.VMEM((TB + NA, 32, P_SIZE), b16),
            pltpu.VMEM((3, NA, P_SIZE, P_SIZE), f32),
            pltpu.VMEM((NA, P_SIZE, P_SIZE), f32),
            pltpu.VMEM((6, NA, P_SIZE), f32),
            pltpu.VMEM((8, NA, P_SIZE), f32),
            pltpu.VMEM((NA * NL, P_SIZE, P_SIZE), f32),
            pltpu.VMEM((NA * NL, P_SIZE, P_SIZE), f32),
            pltpu.VMEM((NA * NL, P_SIZE, P_SIZE), f32),
            pltpu.SemaphoreType.DMA((len(args) + 4,)),
            pltpu.SemaphoreType.DMA((18,)),
        ],
        compiler_params=pltpu.CompilerParams(
            collective_id=0, has_side_effects=True, vmem_limit_bytes=50 * 1024 * 1024
        ),
    )(*args)
    rho, acc = pl.pallas_call(
        late_terms,
        out_shape=results,
        in_specs=[smem] * 2 + [vmem] * 5,
        out_specs=(vmem, vmem),
        compiler_params=pltpu.CompilerParams(vmem_limit_bytes=16 * 1024 * 1024),
    )(masks, near, rho, acc, table, ratios, mine)
    return rho.reshape(-1), acc


def solution(mesh):
    both = ("group", "region")
    placed = (
        P(None, both),
        P(None, both),
        P(both),
        P(both),
        P(both),
        P(both),
        P(both, None),
        P(both),
        P(both, None, None),
        P(both, None, None),
        P(both, None, None),
    )
    return jax.shard_map(
        body,
        mesh=mesh,
        in_specs=placed,
        out_specs=(P(both), P(None, both)),
        check_vma=False,
    )
```
